128 devices in a mesh: queue: 4 (over x_hi, core), ctx: 32 (over x_lo, z, y).
Axes of the slice: x: 4 (x_hi: 2, x_lo: 2; x = x_hi * 2 + x_lo), y: 4, z: 4, core: 2. Of those that a mesh axis runs over, the one named last changes fastest.
Arguments:
- queries: bfloat16 [4, 2048, 32, 128], P('queue', 'ctx'), may hold values from -110 to 110, as said below
- keys: bfloat16 [4, 2048, 32, 128], P('queue', 'ctx'), may hold values from -9 to 9, as said below
- values: bfloat16 [4, 2048, 32, 128], P('queue', 'ctx'), may hold values from -6 to 6
- gate_table: float32 [8, 32, 128], replicated, may hold values from 0.5 to 2
- noise_level: int32 [4], replicated, may hold values from 0 to 7, as said below
- stretch_order: int32 [4], replicated, may hold values from 0 to 3, each once
- block_mask: int32 [4, 4], replicated, may hold values from 0 to 1, as said below
Outputs:
- attended: bfloat16 [4, 2048, 32, 128], P('queue', 'ctx')
The draws below stay inside these ranges and needn't reach their ends.
Inputs may be any that keep to these rules, and one draw needn't show every extreme that they name: queries follow a standard normal law clipped at 4.5, some rows a multiple of up to 24 of a key of the same stretch. keys follow a standard normal law clipped at 4.5, rows scaled by up to 2. `noise_level`: the stretches have pairwise distinct noise levels; level 0 and level 7 are always among them. block_mask[p, p] = 1 and block_mask[p, p - 1] = 1; block_mask[p, q] = 0 for q > p; entries with q < p - 1 are 0 or 1.
All inputs are finite; a program needn't handle non-finite values.
Results may differ from the reference program's by a relative error of at most 0.01.
Values may be sent and summed in bfloat16 or wider, within the bound.
No kernel may reach another device: no remote copies, remote signals or barrier semaphores. Data moves between devices by JAX's collectives and lax.ppermute only.
A program may use at most 192 MiB of HBM per device.

```python
import math
import jax
import jax.numpy as jnp
from jax import lax

HEADS = 32
HD = 128
LEVELS = 8
STRETCH = 2048
STRETCHES = 4


def base_pair(key):
    full_shape = (STRETCHES, STRETCH, HEADS, HD)
    query_base = jnp.clip(jax.random.normal(jax.random.fold_in(key, 101), full_shape, jnp.float32), -4.5, 4.5)
    key_base = jnp.clip(jax.random.normal(jax.random.fold_in(key, 102), full_shape, jnp.float32), -4.5, 4.5)
    return (query_base, key_base)


def draw_queries(key, part):
    query_base, key_base = base_pair(key)
    return query_base.astype(jnp.bfloat16)


def draw_keys(key, part):
    query_base, key_base = base_pair(key)
    return key_base.astype(jnp.bfloat16)


def draw_noise_level(key, part):
    key = jax.random.fold_in(key, 11)
    middle = 1 + jax.random.permutation(jax.random.fold_in(key, 1), LEVELS - 2)[:STRETCHES - 2]
    ends = jnp.array([0, LEVELS - 1], jnp.int32)
    chosen = jnp.concatenate([ends, middle.astype(jnp.int32)])
    placing = jax.random.permutation(jax.random.fold_in(key, 2), STRETCHES)
    return chosen[placing].astype(jnp.int32)


def draw_block_mask(key, part):
    key = jax.random.fold_in(key, 7)
    coins = jax.random.randint(key, (STRETCHES, STRETCHES), 0, 2)
    row_pos = jnp.arange(STRETCHES)[:, None]
    col_pos = jnp.arange(STRETCHES)[None, :]
    near = (col_pos == row_pos) | (col_pos == row_pos - 1)
    return jnp.where(near, 1, jnp.where(col_pos < row_pos, coins, 0)).astype(jnp.int32)


def level_of(key, dims, pieces, smallest, top_value):
    def one(dim, parts):
        draws = jax.random.uniform(jax.random.fold_in(jax.random.fold_in(key, 6), dim), (parts,), jnp.float32, smallest / len(pieces), top_value / len(pieces))
        return jnp.repeat(jnp.exp(draws), dims[dim] // parts).reshape((-1,) + (1,) * (len(dims) - dim - 1))

    level = one(*pieces[0])
    for cut in pieces[1:]:
        level = level * one(*cut)
    return level


def centred(stream_key, dims, width, limit, shards=(), kind=jnp.bfloat16):
    values = width * jax.random.normal(stream_key, dims, jnp.float32)
    if shards:
        values = values * level_of(stream_key, dims, shards, -0.22, 0.18)
    return jnp.clip(values, -limit, limit).astype(kind)


def setup_inputs(seed: int = 0) -> dict:
    key_list = jax.random.split(jax.random.key(seed), 8)
    queries = draw_queries(jax.random.fold_in(key_list[7], 71), 0)
    keys = draw_keys(jax.random.fold_in(key_list[7], 71), 0)
    values = centred(key_list[2], (STRETCHES, STRETCH, HEADS, HD), 1.0, 6.0, ((0, 4), (1, 32)))
    gate_table = jnp.clip(jnp.exp(jax.random.uniform(key_list[3], (LEVELS, HEADS, HD), jnp.float32, math.log(0.5), math.log(2.0))), 0.5, 2.0)
    noise_level = draw_noise_level(jax.random.fold_in(key_list[7], 71), 0)
    stretch_order = jax.random.permutation(key_list[5], STRETCHES).astype(jnp.int32)
    block_mask = draw_block_mask(jax.random.fold_in(key_list[7], 71), 0)
    return {"queries": queries, "keys": keys, "values": values, "gate_table": gate_table, "noise_level": noise_level, "stretch_order": stretch_order, "block_mask": block_mask}


def reference(queries, keys, values, gate_table, noise_level, stretch_order, block_mask):
    stretch_ids = jnp.arange(STRETCHES, dtype=jnp.int32)
    order_hot = (stretch_order[:, None] == stretch_ids[None, :]).astype(jnp.float32)
    mask_float = block_mask.astype(jnp.float32)
    allowed = jnp.dot(jnp.dot(order_hot, mask_float, precision=lax.Precision.HIGHEST), order_hot.T, precision=lax.Precision.HIGHEST)
    level_hot = (noise_level[:, None] == jnp.arange(LEVELS, dtype=jnp.int32)[None, :]).astype(jnp.float32)
    gate_rows = jnp.einsum("cl,lhd->chd", level_hot, gate_table, precision=lax.Precision.HIGHEST)
    keys_all = keys.reshape(STRETCHES * STRETCH, HEADS, HD)
    values_all = values.reshape(STRETCHES * STRETCH, HEADS, HD)
    key_stretch = jnp.arange(STRETCHES * STRETCH, dtype=jnp.int32) // STRETCH
    factor = 1.0 / (HD ** 0.5)

    def one_stretch(stretch_id):
        usable = jnp.dot(allowed[stretch_id], (key_stretch[None, :] == stretch_ids[:, None]).astype(jnp.float32)) > 0.5
        query_rows = queries[stretch_id]

        def one_head(head_id):
            query_head = query_rows[:, head_id, :]
            scores = jnp.dot(query_head, keys_all[:, head_id, :].T, preferred_element_type=jnp.float32) * factor
            scores = jnp.where(usable[None, :], scores, -jnp.inf)
            row_max = jnp.max(scores, axis=1)
            weights = jnp.exp(scores - row_max[:, None])
            total = jnp.sum(weights, axis=1)
            mixed = jnp.dot(weights.astype(jnp.bfloat16), values_all[:, head_id, :], preferred_element_type=jnp.float32)
            return mixed / total[:, None]

        heads_out = lax.map(one_head, jnp.arange(HEADS, dtype=jnp.int32))
        result = jnp.transpose(heads_out, (1, 0, 2)) * gate_rows[stretch_id][None]
        return result.astype(jnp.bfloat16)

    return lax.map(one_stretch, stretch_ids)
```

```python
import functools

import jax
import jax.numpy as jnp
from jax import lax
from jax.experimental import pallas as pl
from jax.experimental.pallas import tpu as pltpu
from jax.sharding import Mesh, PartitionSpec as P

LOG2E = 1.4426950408889634
SWAP = [(0, 1), (1, 0)]


def attend_kernel(
    place, order, levels, mask, own, other, gates, out, q_all, row_max, total, mixed, *, toks, share
):
    core, head = place[0], place[1]
    groups = own.shape[0] // 2
    size = own.shape[-1]
    rows = groups * share
    keys = groups * toks
    scale = LOG2E / size**0.5
    row_max[...] = jnp.full(row_max.shape, -1e30, jnp.float32)
    total[...] = jnp.zeros(total.shape, jnp.float32)
    mixed[...] = jnp.zeros(mixed.shape, jnp.float32)
    start = pl.multiple_of(2 * toks + core * share, 16)

    def stretch_of(slot):
        return 2 * (slot % 2) + jnp.where(slot < 2, core, 1 - core)

    for slot in range(4):
        src = own if slot < 2 else other
        part = src[pl.ds((slot % 2) * groups, groups), pl.ds(start, share), :]
        q_all[slot] = part.reshape(rows, size)

    for key_slot in range(4):
        src = own if key_slot < 2 else other
        key_pos = order[stretch_of(key_slot)]
        lo = (key_slot % 2) * groups

        @pl.loop(0, 4)
        def _(query_slot, src=src, lo=lo, key_pos=key_pos):
            query_pos = order[stretch_of(query_slot)]

            @pl.when(mask[query_pos, key_pos] == 1)
            def _():
                k = src[lo : lo + groups, 0:toks, :].reshape(keys, size)
                v = src[lo : lo + groups, toks : 2 * toks, :].reshape(keys, size)
                sub = 128
                for r in range(0, rows, sub):
                    at = (query_slot, slice(r, r + sub), slice(None))
                    q = q_all[at]
                    s = lax.dot_general(
                        q, k, (((1,), (1,)), ((), ())), preferred_element_type=jnp.float32
                    )
                    old = row_max[at][:, 0:1]
                    new = jnp.maximum(old, jnp.max(s, axis=1, keepdims=True))
                    keep = jnp.exp2((old - new) * scale)
                    p = jnp.exp2((s - new) * scale)
                    row_max[at] = jnp.broadcast_to(new, (sub, size))
                    total[at] = total[at] * keep + jnp.sum(p, axis=1, keepdims=True)
                    mixed[at] = mixed[at] * keep + jnp.dot(
                        p.astype(jnp.bfloat16), v, preferred_element_type=jnp.float32
                    )

    for slot in range(4):
        stretch = stretch_of(slot)
        gate = gates[levels[stretch], pl.ds(head, 1), :]
        result = mixed[slot] / total[slot] * gate
        out[stretch] = result.astype(jnp.bfloat16).reshape(groups, share, size)


def attend(place, order, levels, mask, own, other, gates, toks, share):
    groups, size = own.shape[0] // 2, own.shape[-1]
    rows = groups * share
    smem = pl.BlockSpec(memory_space=pltpu.SMEM)
    vmem = pl.BlockSpec(memory_space=pltpu.VMEM)
    return pl.pallas_call(
        functools.partial(attend_kernel, toks=toks, share=share),
        out_shape=jax.ShapeDtypeStruct((4, groups, share, size), jnp.bfloat16),
        in_specs=[smem, smem, smem, smem, vmem, vmem, vmem],
        out_specs=vmem,
        scratch_shapes=[
            pltpu.VMEM((4, rows, size), jnp.bfloat16),
            pltpu.VMEM((4, rows, size), jnp.float32),
            pltpu.VMEM((4, rows, size), jnp.float32),
            pltpu.VMEM((4, rows, size), jnp.float32),
        ],
        compiler_params=pltpu.CompilerParams(vmem_limit_bytes=48 * 2**20),
    )(place, order, levels, mask, own, other, gates)


def shards(queries, keys, values, gate_table, noise_level, stretch_order, block_mask):
    toks, heads, size = queries.shape[1:]
    half, share = toks // 2, toks // 4
    k = jnp.swapaxes(keys[0], 0, 1)
    v = jnp.swapaxes(values[0], 0, 1)
    q = jnp.swapaxes(queries[0].reshape(2, half, heads, size), 1, 2)
    kv = jnp.concatenate([k, v], axis=1)
    send = jnp.concatenate([jnp.broadcast_to(kv[None], (2,) + kv.shape), q], axis=2)
    send = send.reshape(2 * heads, 2 * toks + half, size)
    own = lax.all_to_all(send, ("xh", "ctx"), 0, 0, tiled=True)
    other = lax.ppermute(own, "core", SWAP)
    place = jnp.stack([lax.axis_index("core"), lax.axis_index("ctx")]).astype(jnp.int32)
    part = attend(place, stretch_order, noise_level, block_mask, own, other, gate_table, toks, share)
    back = lax.all_to_all(
        part.reshape(4 * heads, share, size), ("xh", "core", "ctx"), 0, 0, tiled=True
    )
    back = back.reshape(4, heads, share, size)
    return jnp.swapaxes(back, 1, 2).reshape(1, toks, heads, size)


def solution(mesh):
    wide = Mesh(mesh.devices.reshape(2, 2, -1), ("xh", "core", "ctx"))
    tokens = P(("xh", "core"), "ctx", None, None)
    return jax.shard_map(
        shards,
        mesh=wide,
        in_specs=(tokens, tokens, tokens, P(), P(), P(), P()),
        out_specs=tokens,
        check_vma=False,
    )
```

```python
import functools

import jax
import jax.numpy as jnp
from jax import lax
from jax.experimental import pallas as pl
from jax.experimental.pallas import tpu as pltpu
from jax.sharding import Mesh, PartitionSpec as P

LOG2E = 1.4426950408889634
SWAP = [(0, 1), (1, 0)]


BOTH = (((1,), (1,)), ((), ()))
def attend_kernel(place, order, levels, mask, own, other, gates, out,
           pair_q, pair_k, q_all, k_all, v_all, run_max, total, mixed, s_a, s_b, m_a, m_b, f_a, f_b, *, toks, share, kd, kt):
    core, head = place[0], place[1]
    groups = own.shape[0] // 2
    size = own.shape[-1]
    rows = groups * share
    keys = groups * toks
    scale = LOG2E / size**0.5
    run_max[...] = jnp.full(run_max.shape, -1e30, jnp.float32)
    total[...] = jnp.zeros(total.shape, jnp.float32)
    mixed[...] = jnp.zeros(mixed.shape, jnp.float32)
    start = pl.multiple_of(2 * toks + core * share, 16)
    spot = lax.broadcasted_iota(jnp.int32, (size, size), 0) == lax.broadcasted_iota(jnp.int32, (size, size), 1)
    eye = jnp.where(spot, 1.0, 0.0).astype(jnp.bfloat16)

    def stretch_of(slot):
        return 2 * (slot % 2) + jnp.where(slot < 2, core, 1 - core)

    for slot in range(4):
        src = own if slot < 2 else other
        at = pl.ds((slot % 2) * groups, groups)
        q = src[at, pl.ds(start, share), :].reshape(rows, size).astype(jnp.float32) * scale
        high = q.astype(jnp.bfloat16)
        q_all[slot, :, 0:size] = high
        q_all[slot, :, size:] = (q - high.astype(jnp.float32)).astype(jnp.bfloat16)
        k_all[slot] = src[at, 0:toks, :].reshape(keys, size)
        v = src[at, toks : 2 * toks, :].reshape(keys, size)
        v_all[slot] = lax.dot_general(eye, v, BOTH, preferred_element_type=jnp.float32).astype(jnp.bfloat16)

    count = jnp.int32(0)
    for key_slot in range(4):
        for query_slot in range(4):
            pair_q[count] = query_slot
            pair_k[count] = key_slot
            hit = mask[order[stretch_of(query_slot)], order[stretch_of(key_slot)]] == 1
            count = count + hit.astype(jnp.int32)

    def step(n, s_new, m_new, f_new, s_old, m_old, f_old, fresh=True, used=True):
        if fresh:
            nn = jnp.minimum(n + 1, count - 1)
            qn, kn = pair_q[nn], pair_k[nn]
            q = q_all[qn]
            best = None
        if used:
            qs, ks = pair_q[n], pair_k[n]
            m = m_old[0:1, :]
            f = f_old[0:1, :]
            parts, tots, acc = [], None, None
        for c in range(0, keys, kt):
            if fresh:
                k = k_all[kn, c : c + kt, :]
                s = lax.dot_general(jnp.concatenate([k, k], axis=1), q, BOTH, preferred_element_type=jnp.float32)
                s_new[c : c + kt, :] = s
                top = jnp.max(s.reshape(kt // 8, 8, rows), axis=0)
                best = top if best is None else jnp.maximum(best, top)
            if used:
                p = jnp.exp2(s_old[c : c + kt, :] - m)
                t = jnp.sum(p.reshape(kt // 8, 8, rows), axis=0)
                tots = t if tots is None else tots + t
                parts.append(p.astype(jnp.bfloat16))
                if len(parts) * kt == kd:
                    d = jnp.dot(v_all[ks, :, c + kt - kd : c + kt], jnp.concatenate(parts, axis=0), preferred_element_type=jnp.float32)
                    acc = d if acc is None else acc + d
                    parts = []
        if used:
            total[qs] = total[qs] * f + tots
            mixed[qs] = mixed[qs] * f + acc
        if fresh:
            old = run_max[qn]
            new = jnp.maximum(old, jnp.max(best, axis=0, keepdims=True))
            run_max[qn] = new
            m_new[...] = new
            f_new[...] = jnp.exp2(old - new)

    a, b = (s_a, m_a, f_a), (s_b, m_b, f_b)
    step(-1, *a, *b, used=False)

    @pl.loop(0, (count + 1) // 2)
    def _(t):
        step(2 * t, *b, *a)

        @pl.when(2 * t + 1 < count)
        def _():
            step(2 * t + 1, *a, *b)

    for slot in range(4):
        stretch = stretch_of(slot)
        gate = gates[levels[stretch], pl.ds(head, 1), :]
        o = mixed[slot] / jnp.sum(total[slot], axis=0, keepdims=True)
        out[stretch] = (o.T * gate).astype(jnp.bfloat16).reshape(groups, share, size)

def attend(place, order, levels, mask, own, other, gates, toks, share, kd=512, kt=512):
    groups, size = own.shape[0] // 2, own.shape[-1]
    rows, keys = groups * share, groups*toks
    smem = pl.BlockSpec(memory_space=pltpu.SMEM)
    vmem = pl.BlockSpec(memory_space=pltpu.VMEM)
    f32, bf16 = jnp.float32, jnp.bfloat16
    return pl.pallas_call(
        functools.partial(attend_kernel, toks=toks, share=share, kd=kd, kt=kt),
        out_shape=jax.ShapeDtypeStruct((4, groups, share, size), jnp.bfloat16),
        in_specs=[smem, smem, smem, smem, vmem, vmem, vmem],
        out_specs=vmem,
        scratch_shapes=[
            pltpu.SMEM((17,), jnp.int32), pltpu.SMEM((17,), jnp.int32),
            pltpu.VMEM((4, rows, 2*size), bf16),
            pltpu.VMEM((4, keys, size), bf16),
            pltpu.VMEM((4, size, keys), bf16),
            pltpu.VMEM((4, 8, rows), f32),
            pltpu.VMEM((4, 8, rows), f32),
            pltpu.VMEM((4, size, rows), f32),
            pltpu.VMEM((keys, rows), f32), pltpu.VMEM((keys, rows), f32),
            pltpu.VMEM((8, rows), f32), pltpu.VMEM((8, rows), f32),
            pltpu.VMEM((8, rows), f32), pltpu.VMEM((8, rows), f32),
        ],
        compiler_params=pltpu.CompilerParams(vmem_limit_bytes=48 * 2**20),
    )(place, order, levels, mask, own, other, gates)


def shards(queries, keys, values, gate_table, noise_level, stretch_order, block_mask):
    toks, heads, size = queries.shape[1:]
    half, share = toks // 2, toks // 4
    k = jnp.swapaxes(keys[0], 0, 1)
    v = jnp.swapaxes(values[0], 0, 1)
    q = jnp.swapaxes(queries[0].reshape(2, half, heads, size), 1, 2)
    kv = jnp.concatenate([k, v], axis=1)
    send = jnp.concatenate([jnp.broadcast_to(kv[None], (2,) + kv.shape), q], axis=2)
    send = send.reshape(2 * heads, 2 * toks + half, size)
    own = lax.all_to_all(send, ("xh", "ctx"), 0, 0, tiled=True)
    other = lax.ppermute(own, "core", SWAP)
    place = jnp.stack([lax.axis_index("core"), lax.axis_index("ctx")]).astype(jnp.int32)
    part = attend(place, stretch_order, noise_level, block_mask, own, other, gate_table, toks, share)
    back = lax.all_to_all(
        part.reshape(4 * heads, share, size), ("xh", "core", "ctx"), 0, 0, tiled=True
    )
    back = back.reshape(4, heads, share, size)
    return jnp.swapaxes(back, 1, 2).reshape(1, toks, heads, size)


def solution(mesh):
    wide = Mesh(mesh.devices.reshape(2, 2, -1), ("xh", "core", "ctx"))
    tokens = P(("xh", "core"), "ctx", None, None)
    return jax.shard_map(
        shards,
        mesh=wide,
        in_specs=(tokens, tokens, tokens, P(), P(), P(), P()),
        out_specs=tokens,
        check_vma=False,
    )
```

```python
import functools

import jax
import jax.numpy as jnp
from jax import lax
from jax.experimental import pallas as pl
from jax.experimental.pallas import tpu as pltpu
from jax.sharding import Mesh, PartitionSpec as P

LOG2E = 1.4426950408889634
SWAP = [(0, 1), (1, 0)]
BOTH = (((1,), (1,)), ((), ()))
TILE = 512
SMEM = pl.BlockSpec(memory_space=pltpu.SMEM)
VMEM = pl.BlockSpec(memory_space=pltpu.VMEM)
LIMIT = 48 * 2**20


def pack_kernel(queries, keys, values, send, q_in, k_in, v_in, wide, q_out, k_out, v_out, ins, outs):
    toks, heads, size = queries.shape
    half = toks // 2
    pitch = wide.shape[1] // toks
    parts = ((keys, k_in, k_out), (values, v_in, v_out), (queries, q_in, q_out))
    loads, stores = [], []
    for i, (src, dst, _) in enumerate(parts):
        for h in range(2):
            at = pl.ds(h * half, half)
            loads.append(pltpu.make_async_copy(src.at[at], dst.at[at], ins.at[2 * i + h]))
            loads[-1].start()
    for i, (_, part, turned) in enumerate(parts):
        for h in range(2):
            loads[2 * i + h].wait()
            for tok in range(h * half, (h + 1) * half):
                wide[i, tok * pitch : tok * pitch + heads, :] = part[tok].astype(jnp.float32)
        for head in range(heads):
            x = wide[i, pl.ds(head, toks, stride=pitch), :].astype(jnp.bfloat16)
            if i < 2:
                turned[head] = x
            else:
                turned[0, head] = x[:half]
                turned[1, head] = x[half:]
        for xh in range(2):
            src = turned if i < 2 else turned.at[xh]
            rows = pl.ds(i * toks, toks if i < 2 else half)
            dst = send.at[pl.ds(xh * heads, heads), rows]
            stores.append(pltpu.make_async_copy(src, dst, outs.at[2 * i + xh]))
            stores[-1].start()
    for copy in stores:
        copy.wait()


def pack(queries, keys, values):
    toks, heads, size = queries.shape
    hbm = pl.BlockSpec(memory_space=pl.ANY)
    block = pltpu.VMEM((toks, heads, size), jnp.bfloat16)
    turned = pltpu.VMEM((heads, toks, size), jnp.bfloat16)
    return pl.pallas_call(
        pack_kernel,
        out_shape=jax.ShapeDtypeStruct((2 * heads, 2 * toks + toks // 2, size), jnp.bfloat16),
        in_specs=[hbm, hbm, hbm],
        out_specs=hbm,
        scratch_shapes=[
            block,
            block,
            block,
            pltpu.VMEM((3, toks * (heads + 1), size), jnp.float32),
            pltpu.VMEM((2, heads, toks // 2, size), jnp.bfloat16),
            turned,
            turned,
            pltpu.SemaphoreType.DMA((6,)),
            pltpu.SemaphoreType.DMA((6,)),
        ],
        compiler_params=pltpu.CompilerParams(vmem_limit_bytes=60 * 2**20),
    )(queries, keys, values)


def stretch_of(slot, core):
    return 2 * (slot % 2) + jnp.where(slot < 2, core, 1 - core)


def load_slot(src, slot, core, toks, share, q_all, k_all):
    groups, size = src.shape[0] // 2, src.shape[-1]
    at = pl.ds((slot % 2) * groups, groups)
    start = pl.multiple_of(2 * toks + core * share, 16)
    q = src[at, pl.ds(start, share), :].reshape(groups * share, size).astype(jnp.float32)
    q = q * (LOG2E / size**0.5)
    high = q.astype(jnp.bfloat16)
    q_all[slot, :, 0:size] = high
    q_all[slot, :, size:] = (q - high.astype(jnp.float32)).astype(jnp.bfloat16)
    k_all[slot] = src[at, 0:toks, :].reshape(groups * toks, size)


def turn_values(src, slot, toks):
    groups, size = src.shape[0] // 2, src.shape[-1]
    row = lax.broadcasted_iota(jnp.int32, (size, size), 0)
    col = lax.broadcasted_iota(jnp.int32, (size, size), 1)
    eye = jnp.where(row == col, 1.0, 0.0).astype(jnp.bfloat16)
    v = src[pl.ds((slot % 2) * groups, groups), toks : 2 * toks, :].reshape(groups * toks, size)
    turned = lax.dot_general(eye, v, BOTH, preferred_element_type=jnp.float32)
    return turned.astype(jnp.bfloat16)


def run_pairs(slots, core, order, mask, pair_q, pair_k, q_all, k_all, v_all, state, bufs):
    run_max, total, mixed = state
    s_a, s_b, m_a, m_b, f_a, f_b = bufs
    keys, rows = s_a.shape
    count = jnp.int32(0)
    for query_slot, key_slot in slots:
        pair_q[count] = query_slot
        pair_k[count] = key_slot
        query_pos = order[stretch_of(query_slot, core)]
        key_pos = order[stretch_of(key_slot, core)]
        count = count + (mask[query_pos, key_pos] == 1).astype(jnp.int32)

    def step(n, s_new, m_new, f_new, s_old, m_old, f_old, used=True):
        later = jnp.minimum(n + 1, count - 1)
        next_q, next_k = pair_q[later], pair_k[later]
        q = q_all[next_q]
        best = sums = acc = None
        if used:
            now_q, now_k = pair_q[n], pair_k[n]
            m, f = m_old[0:1, :], f_old[0:1, :]
        for c in range(0, keys, TILE):
            k = k_all[next_k, c : c + TILE, :]
            s = lax.dot_general(
                jnp.concatenate([k, k], axis=1), q, BOTH, preferred_element_type=jnp.float32
            )
            s_new[c : c + TILE, :] = s
            top = jnp.max(s.reshape(TILE // 8, 8, rows), axis=0)
            best = top if best is None else jnp.maximum(best, top)
            if used:
                p = jnp.exp2(s_old[c : c + TILE, :] - m)
                t = jnp.sum(p.reshape(TILE // 8, 8, rows), axis=0)
                d = jnp.dot(
                    v_all[now_k, :, c : c + TILE],
                    p.astype(jnp.bfloat16),
                    preferred_element_type=jnp.float32,
                )
                sums = t if sums is None else sums + t
                acc = d if acc is None else acc + d
        if used:
            total[now_q] = total[now_q] * f + sums
            mixed[now_q] = mixed[now_q] * f + acc
        old = run_max[next_q]
        new = jnp.maximum(old, jnp.max(best, axis=0, keepdims=True))
        run_max[next_q] = new
        m_new[...] = new
        f_new[...] = jnp.exp2(old - new)

    a, b = (s_a, m_a, f_a), (s_b, m_b, f_b)
    step(-1, *a, *b, used=False)

    @pl.loop(0, (count + 1) // 2)
    def _(t):
        step(2 * t, *b, *a)

        @pl.when(2 * t + 1 < count)
        def _():
            step(2 * t + 1, *a, *b)


def clear(run_max, total, mixed):
    run_max[...] = jnp.full(run_max.shape, -1e30, jnp.float32)
    total[...] = jnp.zeros(total.shape, jnp.float32)
    mixed[...] = jnp.zeros(mixed.shape, jnp.float32)


def first_kernel(
    place, order, mask, own, run_max, total, mixed, v_all, pair_q, pair_k, q_all, k_all, *bufs, toks, share
):
    core = place[0]
    clear(run_max, total, mixed)
    for slot in range(2):
        load_slot(own, slot, core, toks, share, q_all, k_all)
        v_all[slot] = turn_values(own, slot, toks)
    slots = [(q, k) for q in range(2) for k in range(2)]
    state = (run_max, total, mixed)
    run_pairs(slots, core, order, mask, pair_q, pair_k, q_all, k_all, v_all, state, bufs)


def rest_kernel(
    place, order, levels, mask, own, other, gates, max_in, total_in, mixed_in, v_in, out,
    pair_q, pair_k, q_all, k_all, v_all, run_max, total, mixed, *bufs, toks, share
):
    core, head = place[0], place[1]
    clear(run_max.at[2:4], total.at[2:4], mixed.at[2:4])
    run_max[0:2] = max_in[...]
    total[0:2] = total_in[...]
    mixed[0:2] = mixed_in[...]
    v_all[0:2] = v_in[...]
    for slot in range(4):
        load_slot(own if slot < 2 else other, slot, core, toks, share, q_all, k_all)
        if slot >= 2:
            v_all[slot] = turn_values(other, slot, toks)
    slots = [(q, k) for k in range(4) for q in range(4) if q >= 2 or k >= 2]
    state = (run_max, total, mixed)
    run_pairs(slots, core, order, mask, pair_q, pair_k, q_all, k_all, v_all, state, bufs)
    groups, size = own.shape[0] // 2, own.shape[-1]
    for slot in range(4):
        stretch = stretch_of(slot, core)
        gate = gates[levels[stretch], pl.ds(head, 1), :]
        o = mixed[slot] / jnp.sum(total[slot], axis=0, keepdims=True)
        out[stretch] = (o.T * gate).astype(jnp.bfloat16).reshape(groups, share, size)


def state_of(n, rows, size):
    return [(n, 8, rows), (n, 8, rows), (n, size, rows)]


def scratch(n, rows, keys, size):
    f32, bf16 = jnp.float32, jnp.bfloat16
    head = [
        pltpu.SMEM((17,), jnp.int32),
        pltpu.SMEM((17,), jnp.int32),
        pltpu.VMEM((n, rows, 2 * size), bf16),
        pltpu.VMEM((n, keys, size), bf16),
    ]
    bufs = [pltpu.VMEM((keys, rows), f32)] * 2 + [pltpu.VMEM((8, rows), f32)] * 4
    return head, bufs


def first(place, order, mask, own, toks, share):
    groups, size = own.shape[0] // 2, own.shape[-1]
    rows, keys = groups * share, groups * toks
    head, bufs = scratch(2, rows, keys, size)
    shapes = [jax.ShapeDtypeStruct(s, jnp.float32) for s in state_of(2, rows, size)]
    shapes.append(jax.ShapeDtypeStruct((2, size, keys), jnp.bfloat16))
    return pl.pallas_call(
        functools.partial(first_kernel, toks=toks, share=share),
        out_shape=shapes,
        in_specs=[SMEM, SMEM, SMEM, VMEM],
        out_specs=[VMEM] * 4,
        scratch_shapes=head + bufs,
        compiler_params=pltpu.CompilerParams(vmem_limit_bytes=LIMIT),
        cost_estimate=pl.CostEstimate(
            flops=3 * 4 * rows * keys * size,
            bytes_accessed=8 * 2**20,
            transcendentals=3 * rows * keys,
        ),
    )(place, order, mask, own)


def rest(place, order, levels, mask, own, other, gates, state, toks, share):
    groups, size = own.shape[0] // 2, own.shape[-1]
    rows, keys = groups * share, groups * toks
    head, bufs = scratch(4, rows, keys, size)
    mine = [pltpu.VMEM((4, size, keys), jnp.bfloat16)]
    mine += [pltpu.VMEM(s, jnp.float32) for s in state_of(4, rows, size)]
    return pl.pallas_call(
        functools.partial(rest_kernel, toks=toks, share=share),
        out_shape=jax.ShapeDtypeStruct((4, groups, share, size), jnp.bfloat16),
        in_specs=[SMEM] * 4 + [VMEM] * 7,
        out_specs=VMEM,
        scratch_shapes=head + mine + bufs,
        compiler_params=pltpu.CompilerParams(vmem_limit_bytes=LIMIT),
    )(place, order, levels, mask, own, other, gates, *state)


def shards(queries, keys, values, gate_table, noise_level, stretch_order, block_mask):
    toks, heads, size = queries.shape[1:]
    share = toks // 4
    own = lax.all_to_all(pack(queries[0], keys[0], values[0]), ("xh", "ctx"), 0, 0, tiled=True)
    other = lax.ppermute(own, "core", SWAP)
    place = jnp.stack([lax.axis_index("core"), lax.axis_index("ctx")]).astype(jnp.int32)
    state = first(place, stretch_order, block_mask, own, toks, share)
    part = rest(
        place, stretch_order, noise_level, block_mask, own, other, gate_table, state, toks, share
    )
    back = lax.all_to_all(
        part.reshape(4 * heads, share, size), ("xh", "core", "ctx"), 0, 0, tiled=True
    )
    back = back.reshape(4, heads, share, size)
    return jnp.swapaxes(back, 1, 2).reshape(1, toks, heads, size)


def solution(mesh):
    wide = Mesh(mesh.devices.reshape(2, 2, -1), ("xh", "core", "ctx"))
    tokens = P(("xh", "core"), "ctx", None, None)
    return jax.shard_map(
        shards,
        mesh=wide,
        in_specs=(tokens, tokens, tokens, P(), P(), P(), P()),
        out_specs=tokens,
        check_vma=False,
    )
```

```python
import functools

import jax
import jax.numpy as jnp
from jax import lax
from jax.experimental import pallas as pl
from jax.experimental.pallas import tpu as pltpu
from jax.sharding import Mesh, PartitionSpec as P

LOG2E = 1.4426950408889634
SWAP = [(0, 1), (1, 0)]
BOTH = (((1,), (1,)), ((), ()))
TILE = 512
SMEM = pl.BlockSpec(memory_space=pltpu.SMEM)
VMEM = pl.BlockSpec(memory_space=pltpu.VMEM)
LIMIT = 48 * 2**20


def pack_kernel(queries, keys, values, send, q_in, k_in, v_in, wide, q_out, k_out, v_out, ins, outs):
    toks, heads, size = queries.shape
    half = toks // 2
    pitch = wide.shape[1] // toks
    parts = ((keys, k_in, k_out), (values, v_in, v_out), (queries, q_in, q_out))
    loads, stores = [], []
    for i, (src, dst, _) in enumerate(parts):
        for h in range(2):
            at = pl.ds(h * half, half)
            loads.append(pltpu.make_async_copy(src.at[at], dst.at[at], ins.at[2 * i + h]))
            loads[-1].start()
    for i, (_, part, turned) in enumerate(parts):
        for h in range(2):
            loads[2 * i + h].wait()
            for tok in range(h * half, (h + 1) * half):
                wide[i, tok * pitch : tok * pitch + heads, :] = part[tok].astype(jnp.float32)
        for head in range(heads):
            x = wide[i, pl.ds(head, toks, stride=pitch), :].astype(jnp.bfloat16)
            if i < 2:
                turned[head] = x
            else:
                turned[0, head] = x[:half]
                turned[1, head] = x[half:]
        for xh in range(2):
            src = turned if i < 2 else turned.at[xh]
            rows = pl.ds(i * toks, toks if i < 2 else half)
            dst = send.at[pl.ds(xh * heads, heads), rows]
            stores.append(pltpu.make_async_copy(src, dst, outs.at[2 * i + xh]))
            stores[-1].start()
    for copy in stores:
        copy.wait()


def pack(queries, keys, values):
    toks, heads, size = queries.shape
    hbm = pl.BlockSpec(memory_space=pl.ANY)
    block = pltpu.VMEM((toks, heads, size), jnp.bfloat16)
    turned = pltpu.VMEM((heads, toks, size), jnp.bfloat16)
    return pl.pallas_call(
        pack_kernel,
        out_shape=jax.ShapeDtypeStruct((2 * heads, 2 * toks + toks // 2, size), jnp.bfloat16),
        in_specs=[hbm, hbm, hbm],
        out_specs=hbm,
        scratch_shapes=[
            block,
            block,
            block,
            pltpu.VMEM((3, toks * (heads + 1), size), jnp.float32),
            pltpu.VMEM((2, heads, toks // 2, size), jnp.bfloat16),
            turned,
            turned,
            pltpu.SemaphoreType.DMA((6,)),
            pltpu.SemaphoreType.DMA((6,)),
        ],
        compiler_params=pltpu.CompilerParams(vmem_limit_bytes=60 * 2**20),
    )(queries, keys, values)


def stretch_of(slot, core):
    return 2 * (slot % 2) + jnp.where(slot < 2, core, 1 - core)


def load_queries(q, slot, q_all):
    groups, share, size = q.shape
    q = q.reshape(groups * share, size).astype(jnp.float32) * (LOG2E / size**0.5)
    high = q.astype(jnp.bfloat16)
    q_all[slot, :, 0:size] = high
    q_all[slot, :, size:] = (q - high.astype(jnp.float32)).astype(jnp.bfloat16)


def load_own(own, core, toks, share, q_all, k_all):
    groups = own.shape[0] // 2
    start = pl.multiple_of(2 * toks + core * share, 16)
    for slot in range(2):
        at = slice(slot * groups, (slot + 1) * groups)
        load_queries(own[at, pl.ds(start, share), :], slot, q_all)
        k_all[slot] = own[at, 0:toks, :]


def turn(v):
    groups, toks, size = v.shape
    return v.reshape(groups * toks, size).T


def make_step(q_all, k_all, v_all, state, keys):
    run_max, total, mixed = state
    rows, size = q_all.shape[1], k_all.shape[-1]
    toks = k_all.shape[2]

    def step(fresh, new, used, old):
        best = sums = acc = None
        if used is not None:
            s_old, m_old, f_old = old
            now_q, now_k = used
            m, f = m_old[0:1, :], f_old[0:1, :]
        if fresh is not None:
            s_new, m_new, f_new = new
            next_q, next_k = fresh
            q = q_all[next_q]
        for c in range(0, keys, TILE):
            if fresh is not None:
                k = k_all[next_k, c // toks : (c + TILE) // toks].reshape(TILE, size)
                s = lax.dot_general(
                    jnp.concatenate([k, k], axis=1), q, BOTH, preferred_element_type=jnp.float32
                )
                s_new[c : c + TILE, :] = s
                top = jnp.max(s.reshape(TILE // 8, 8, rows), axis=0)
                best = top if best is None else jnp.maximum(best, top)
            if used is not None:
                p = jnp.exp2(s_old[c : c + TILE, :] - m)
                t = jnp.sum(p.reshape(TILE // 8, 8, rows), axis=0)
                d = jnp.dot(
                    v_all[now_k, :, c : c + TILE],
                    p.astype(jnp.bfloat16),
                    preferred_element_type=jnp.float32,
                )
                sums = t if sums is None else sums + t
                acc = d if acc is None else acc + d
        if used is not None:
            total[now_q] = total[now_q] * f + sums
            mixed[now_q] = mixed[now_q] * f + acc
        if fresh is not None:
            before = run_max[next_q]
            after = jnp.maximum(before, jnp.max(best, axis=0, keepdims=True))
            run_max[next_q] = after
            m_new[...] = after
            f_new[...] = jnp.exp2(before - after)

    return step


def clear(run_max, total, mixed):
    run_max[...] = jnp.full(run_max.shape, -1e30, jnp.float32)
    total[...] = jnp.zeros(total.shape, jnp.float32)
    mixed[...] = jnp.zeros(mixed.shape, jnp.float32)


def first_kernel(
    place, order, mask, own, run_max, total, mixed, v_all, q_all, k_all, *bufs, toks, share
):
    core = place[0]
    groups = own.shape[0] // 2
    clear(run_max, total, mixed)
    load_own(own, core, toks, share, q_all, k_all)
    step = make_step(q_all, k_all, v_all, (run_max, total, mixed), groups * toks)
    a, b = bufs[0::2], bufs[1::2]
    step((0, 0), a, None, None)
    for slot in range(2):
        v_all[slot] = turn(own[slot * groups : (slot + 1) * groups, toks : 2 * toks, :])
    step((1, 1), b, (0, 0), a)
    here, there = order[stretch_of(0, core)], order[stretch_of(1, core)]
    later = jnp.where(here > there, 0, 1)
    cross = (later, 1 - later)
    crossed = mask[jnp.maximum(here, there), jnp.minimum(here, there)] == 1

    @pl.when(crossed)
    def _():
        step(cross, a, (1, 1), b)
        step(None, None, cross, a)

    @pl.when(jnp.logical_not(crossed))
    def _():
        step(None, None, (1, 1), b)


def rest_kernel(
    place, order, levels, mask, own, other, gates, max_in, total_in, mixed_in, v_in, out,
    pair_q, pair_k, sems, q_raw, v_raw, q_all, k_all, v_all, run_max, total, mixed, *bufs, toks, share
):
    core, head = place[0], place[1]
    groups, size = own.shape[0] // 2, own.shape[-1]
    start = pl.multiple_of(2 * toks + core * share, 16)
    copies = []
    for slot in range(2):
        at = pl.ds(slot * groups, groups)
        for rows, dst in (
            (pl.ds(0, toks), k_all.at[2 + slot]),
            (pl.ds(start, share), q_raw.at[slot]),
            (pl.ds(toks, toks), v_raw.at[slot]),
        ):
            copy = pltpu.make_async_copy(other.at[at, rows], dst, sems.at[len(copies)])
            copy.start()
            copies.append(copy)
    clear(run_max.at[2:4], total.at[2:4], mixed.at[2:4])
    run_max[0:2] = max_in[...]
    total[0:2] = total_in[...]
    mixed[0:2] = mixed_in[...]
    v_all[0:2] = v_in[...]
    load_own(own, core, toks, share, q_all, k_all)

    count = jnp.int32(0)
    slots = [(2, 2)] + [(q, k) for k in range(4) for q in range(4) if max(q, k) > 1]
    for i, (query_slot, key_slot) in enumerate(slots):
        pair_q[count] = query_slot
        pair_k[count] = key_slot
        query_pos = order[stretch_of(query_slot, core)]
        key_pos = order[stretch_of(key_slot, core)]
        fits = mask[query_pos, key_pos] == 1
        if i == 0:
            fits = jnp.bool_(True)
        elif (query_slot, key_slot) == (2, 2):
            fits = jnp.bool_(False)
        count = count + fits.astype(jnp.int32)

    step = make_step(q_all, k_all, v_all, (run_max, total, mixed), groups * toks)
    a, b = bufs[0::2], bufs[1::2]

    def pair(n):
        return pair_q[n], pair_k[n]

    for slot in range(2):
        copies[3 * slot].wait()
        copies[3 * slot + 1].wait()
        load_queries(q_raw[slot], 2 + slot, q_all)
    for slot in range(2):
        copies[3 * slot + 2].wait()
    step((2, 2), a, None, None)
    for slot in range(2):
        v_all[2 + slot] = turn(v_raw[slot])

    steps = count - 1

    @pl.loop(0, steps // 2)
    def _(t):
        step(pair(2 * t + 1), b, pair(2 * t), a)
        step(pair(2 * t + 2), a, pair(2 * t + 1), b)

    @pl.when(steps % 2 == 1)
    def _():
        step(pair(steps), b, pair(steps - 1), a)
        step(None, None, pair(steps), b)

    @pl.when(steps % 2 == 0)
    def _():
        step(None, None, pair(steps), a)

    for slot in range(4):
        stretch = stretch_of(slot, core)
        gate = gates[levels[stretch], pl.ds(head, 1), :]
        o = mixed[slot] / jnp.sum(total[slot], axis=0, keepdims=True)
        out[stretch] = (o.T * gate).astype(jnp.bfloat16).reshape(groups, share, size)


def state_of(n, rows, size):
    return [(n, 8, rows), (n, 8, rows), (n, size, rows)]


def scratch(n, groups, toks, share, size):
    f32, bf16 = jnp.float32, jnp.bfloat16
    rows, keys = groups * share, groups * toks
    head = [pltpu.VMEM((n, rows, 2 * size), bf16), pltpu.VMEM((n, groups, toks, size), bf16)]
    bufs = [pltpu.VMEM((keys, rows), f32)] * 2 + [pltpu.VMEM((8, rows), f32)] * 4
    return head, bufs


def first(place, order, mask, own, toks, share):
    groups, size = own.shape[0] // 2, own.shape[-1]
    rows, keys = groups * share, groups * toks
    head, bufs = scratch(2, groups, toks, share, size)
    shapes = [jax.ShapeDtypeStruct(s, jnp.float32) for s in state_of(2, rows, size)]
    shapes.append(jax.ShapeDtypeStruct((2, size, keys), jnp.bfloat16))
    return pl.pallas_call(
        functools.partial(first_kernel, toks=toks, share=share),
        out_shape=shapes,
        in_specs=[SMEM, SMEM, SMEM, VMEM],
        out_specs=[VMEM] * 4,
        scratch_shapes=head + bufs,
        compiler_params=pltpu.CompilerParams(vmem_limit_bytes=LIMIT),
        cost_estimate=pl.CostEstimate(
            flops=3 * 4 * rows * keys * size,
            bytes_accessed=8 * 2**20,
            transcendentals=3 * rows * keys,
        ),
    )(place, order, mask, own)


def rest(place, order, levels, mask, own, other, gates, state, toks, share):
    groups, size = own.shape[0] // 2, own.shape[-1]
    rows, keys = groups * share, groups * toks
    head, bufs = scratch(4, groups, toks, share, size)
    lists = [
        pltpu.SMEM((17,), jnp.int32),
        pltpu.SMEM((17,), jnp.int32),
        pltpu.SemaphoreType.DMA((6,)),
        pltpu.VMEM((2, groups, share, size), jnp.bfloat16),
        pltpu.VMEM((2, groups, toks, size), jnp.bfloat16),
    ]
    mine = [pltpu.VMEM((4, size, keys), jnp.bfloat16)]
    mine += [pltpu.VMEM(s, jnp.float32) for s in state_of(4, rows, size)]
    return pl.pallas_call(
        functools.partial(rest_kernel, toks=toks, share=share),
        out_shape=jax.ShapeDtypeStruct((4, groups, share, size), jnp.bfloat16),
        in_specs=[SMEM] * 4 + [VMEM, pl.BlockSpec(memory_space=pl.ANY)] + [VMEM] * 5,
        out_specs=VMEM,
        scratch_shapes=lists + head + mine + bufs,
        compiler_params=pltpu.CompilerParams(vmem_limit_bytes=LIMIT),
    )(place, order, levels, mask, own, other, gates, *state)


def shards(queries, keys, values, gate_table, noise_level, stretch_order, block_mask):
    toks, heads, size = queries.shape[1:]
    share = toks // 4
    own = lax.all_to_all(pack(queries[0], keys[0], values[0]), ("xh", "ctx"), 0, 0, tiled=True)
    other = lax.ppermute(own, "core", SWAP)
    place = jnp.stack([lax.axis_index("core"), lax.axis_index("ctx")]).astype(jnp.int32)
    state = first(place, stretch_order, block_mask, own, toks, share)
    part = rest(
        place, stretch_order, noise_level, block_mask, own, other, gate_table, state, toks, share
    )
    back = lax.all_to_all(
        part.reshape(4 * heads, share, size), ("xh", "core", "ctx"), 0, 0, tiled=True
    )
    back = back.reshape(4, heads, share, size)
    return jnp.swapaxes(back, 1, 2).reshape(1, toks, heads, size)


def solution(mesh):
    wide = Mesh(mesh.devices.reshape(2, 2, -1), ("xh", "core", "ctx"))
    tokens = P(("xh", "core"), "ctx", None, None)
    return jax.shard_map(
        shards,
        mesh=wide,
        in_specs=(tokens, tokens, tokens, P(), P(), P(), P()),
        out_specs=tokens,
        check_vma=False,
    )
```

```python
import functools

import jax
import jax.numpy as jnp
from jax import lax
from jax.experimental import pallas as pl
from jax.experimental.pallas import tpu as pltpu
from jax.sharding import Mesh, PartitionSpec as P

LOG2E = 1.4426950408889634
SWAP = [(0, 1), (1, 0)]
BOTH = (((1,), (1,)), ((), ()))
TILE = 512
SMEM = pl.BlockSpec(memory_space=pltpu.SMEM)
VMEM = pl.BlockSpec(memory_space=pltpu.VMEM)
LIMIT = 48 * 2**20


def pack_kernel(queries, keys, values, send, q_in, k_in, v_in, wide, q_out, k_out, v_out, ins, outs):
    toks, heads, size = queries.shape
    half = toks // 2
    pitch = wide.shape[1] // toks
    parts = ((keys, k_in, k_out), (values, v_in, v_out), (queries, q_in, q_out))
    loads, stores = [], []
    for i, (src, dst, _) in enumerate(parts):
        for h in range(2):
            at = pl.ds(h * half, half)
            loads.append(pltpu.make_async_copy(src.at[at], dst.at[at], ins.at[2 * i + h]))
            loads[-1].start()
    for i, (_, part, turned) in enumerate(parts):
        for h in range(2):
            loads[2 * i + h].wait()
            for tok in range(h * half, (h + 1) * half):
                wide[i, tok * pitch : tok * pitch + heads, :] = part[tok].astype(jnp.float32)
        for head in range(heads):
            x = wide[i, pl.ds(head, toks, stride=pitch), :].astype(jnp.bfloat16)
            if i < 2:
                turned[head] = x
            else:
                turned[0, head] = x[:half]
                turned[1, head] = x[half:]
        for xh in range(2):
            src = turned if i < 2 else turned.at[xh]
            rows = pl.ds(i * toks, toks if i < 2 else half)
            dst = send.at[pl.ds(xh * heads, heads), rows]
            stores.append(pltpu.make_async_copy(src, dst, outs.at[2 * i + xh]))
            stores[-1].start()
    for copy in stores:
        copy.wait()


def pack(queries, keys, values):
    toks, heads, size = queries.shape
    hbm = pl.BlockSpec(memory_space=pl.ANY)
    block = pltpu.VMEM((toks, heads, size), jnp.bfloat16)
    turned = pltpu.VMEM((heads, toks, size), jnp.bfloat16)
    return pl.pallas_call(
        pack_kernel,
        out_shape=jax.ShapeDtypeStruct((2 * heads, 2 * toks + toks // 2, size), jnp.bfloat16),
        in_specs=[hbm, hbm, hbm],
        out_specs=hbm,
        scratch_shapes=[
            block,
            block,
            block,
            pltpu.VMEM((3, toks * (heads + 1), size), jnp.float32),
            pltpu.VMEM((2, heads, toks // 2, size), jnp.bfloat16),
            turned,
            turned,
            pltpu.SemaphoreType.DMA((6,)),
            pltpu.SemaphoreType.DMA((6,)),
        ],
        compiler_params=pltpu.CompilerParams(vmem_limit_bytes=60 * 2**20),
    )(queries, keys, values)


def stretch_of(slot, core):
    return 2 * (slot % 2) + jnp.where(slot < 2, core, 1 - core)


def load_queries(q, slot, q_all):
    groups, share, size = q.shape
    q_all[slot] = q.reshape(groups * share, size)


def load_own(own, core, toks, share, q_all, k_all):
    groups = own.shape[0] // 2
    start = pl.multiple_of(2 * toks + core * share, 16)
    for slot in range(2):
        at = slice(slot * groups, (slot + 1) * groups)
        load_queries(own[at, pl.ds(start, share), :], slot, q_all)
        k_all[slot] = own[at, 0:toks, :]


def turn(v):
    groups, toks, size = v.shape
    return v.reshape(groups * toks, size).T


def make_step(q_all, k_all, v_all, state, keys):
    run_max, total, mixed = state
    rows, size = q_all.shape[1], k_all.shape[-1]
    toks = k_all.shape[2]
    scale = LOG2E / size**0.5

    def step(fresh, new, used, old):
        best = acc = None
        if used is not None:
            s_old, m_old, f_old = old
            now_q, now_k = used
            m, f = m_old[0:1, :], f_old[0:1, :]
        if fresh is not None:
            s_new, m_new, f_new = new
            next_q, next_k = fresh
            q = q_all[next_q]
        for c in range(0, keys, TILE):
            if fresh is not None:
                k = k_all[next_k, c // toks : (c + TILE) // toks].reshape(TILE, size)
                s = lax.dot_general(
                    k, q, BOTH, preferred_element_type=jnp.float32
                )
                s_new[c : c + TILE, :] = s
                top = jnp.max(s.reshape(TILE // 8, 8, rows), axis=0)
                best = top if best is None else jnp.maximum(best, top)
            if used is not None:
                p = jnp.exp2(s_old[c : c + TILE, :] * scale - m)
                d = jnp.dot(
                    v_all[now_k, :, c : c + TILE],
                    p.astype(jnp.bfloat16),
                    preferred_element_type=jnp.float32,
                )
                acc = d if acc is None else acc + d
        if used is not None:
            total[now_q] = total[now_q] * f + acc[size : size + 8]
            mixed[now_q] = mixed[now_q] * f + acc[:size]
        if fresh is not None:
            before = run_max[next_q]
            after = jnp.maximum(before, jnp.max(best, axis=0, keepdims=True))
            run_max[next_q] = after
            m_new[...] = after * scale
            f_new[...] = jnp.exp2((before - after) * scale)

    return step


def clear(run_max, total, mixed):
    run_max[...] = jnp.full(run_max.shape, -1e30, jnp.float32)
    total[...] = jnp.zeros(total.shape, jnp.float32)
    mixed[...] = jnp.zeros(mixed.shape, jnp.float32)


def first_kernel(
    place, order, mask, own, run_max, total, mixed, v_all, q_all, k_all, *bufs, toks, share
):
    core = place[0]
    groups, size = own.shape[0] // 2, own.shape[-1]
    clear(run_max, total, mixed)
    load_own(own, core, toks, share, q_all, k_all)
    step = make_step(q_all, k_all, v_all, (run_max, total, mixed), groups * toks)
    a, b = bufs[0::2], bufs[1::2]
    v_all[:, size:] = jnp.ones((2, 16, groups * toks), jnp.bfloat16)
    step((0, 0), a, None, None)
    for slot in range(2):
        v_all[slot, :size] = turn(own[slot * groups : (slot + 1) * groups, toks : 2 * toks, :])
    step((1, 1), b, (0, 0), a)
    here, there = order[stretch_of(0, core)], order[stretch_of(1, core)]
    later = jnp.where(here > there, 0, 1)
    cross = (later, 1 - later)
    crossed = mask[jnp.maximum(here, there), jnp.minimum(here, there)] == 1

    @pl.when(crossed)
    def _():
        step(cross, a, (1, 1), b)
        step(None, None, cross, a)

    @pl.when(jnp.logical_not(crossed))
    def _():
        step(None, None, (1, 1), b)


def rest_kernel(
    place, order, levels, mask, own, other, gates, max_in, total_in, mixed_in, v_in, out,
    pair_q, pair_k, sems, q_raw, v_raw, q_all, k_all, v_all, run_max, total, mixed, *bufs, toks, share
):
    core, head = place[0], place[1]
    groups, size = own.shape[0] // 2, own.shape[-1]
    start = pl.multiple_of(2 * toks + core * share, 16)
    copies = []
    for slot in range(2):
        at = pl.ds(slot * groups, groups)
        for rows, dst in (
            (pl.ds(0, toks), k_all.at[2 + slot]),
            (pl.ds(start, share), q_raw.at[slot]),
            (pl.ds(toks, toks), v_raw.at[slot]),
        ):
            copy = pltpu.make_async_copy(other.at[at, rows], dst, sems.at[len(copies)])
            copy.start()
            copies.append(copy)
    clear(run_max.at[2:4], total.at[2:4], mixed.at[2:4])
    run_max[0:2] = max_in[...]
    total[0:2] = total_in[...]
    mixed[0:2] = mixed_in[...]
    v_all[0:2] = v_in[...]
    load_own(own, core, toks, share, q_all, k_all)

    count = jnp.int32(0)
    slots = [(2, 2)] + [(q, k) for k in range(4) for q in range(4) if max(q, k) > 1]
    for i, (query_slot, key_slot) in enumerate(slots):
        pair_q[count] = query_slot
        pair_k[count] = key_slot
        query_pos = order[stretch_of(query_slot, core)]
        key_pos = order[stretch_of(key_slot, core)]
        fits = mask[query_pos, key_pos] == 1
        if i == 0:
            fits = jnp.bool_(True)
        elif (query_slot, key_slot) == (2, 2):
            fits = jnp.bool_(False)
        count = count + fits.astype(jnp.int32)

    step = make_step(q_all, k_all, v_all, (run_max, total, mixed), groups * toks)
    a, b = bufs[0::2], bufs[1::2]

    def pair(n):
        return pair_q[n], pair_k[n]

    for copy in copies[0:2]:
        copy.wait()
    load_queries(q_raw[0], 2, q_all)
    v_all[2:4, size:] = jnp.ones((2, 16, groups * toks), jnp.bfloat16)
    step((2, 2), a, None, None)
    for copy in copies[2:]:
        copy.wait()
    load_queries(q_raw[1], 3, q_all)
    for slot in range(2):
        v_all[2 + slot, :size] = turn(v_raw[slot])

    steps = count - 1

    @pl.loop(0, steps // 2)
    def _(t):
        step(pair(2 * t + 1), b, pair(2 * t), a)
        step(pair(2 * t + 2), a, pair(2 * t + 1), b)

    @pl.when(steps % 2 == 1)
    def _():
        step(pair(steps), b, pair(steps - 1), a)
        step(None, None, pair(steps), b)

    @pl.when(steps % 2 == 0)
    def _():
        step(None, None, pair(steps), a)

    for slot in range(4):
        stretch = stretch_of(slot, core)
        gate = gates[levels[stretch], pl.ds(head, 1), :]
        o = mixed[slot] / total[slot, 0:1, :]
        out[stretch] = (o.T * gate).astype(jnp.bfloat16).reshape(groups, share, size)


def state_of(n, rows, size):
    return [(n, 8, rows), (n, 8, rows), (n, size, rows)]


def scratch(n, groups, toks, share, size):
    f32, bf16 = jnp.float32, jnp.bfloat16
    rows, keys = groups * share, groups * toks
    head = [pltpu.VMEM((n, rows, size), bf16), pltpu.VMEM((n, groups, toks, size), bf16)]
    bufs = [pltpu.VMEM((keys, rows), f32)] * 2 + [pltpu.VMEM((8, rows), f32)] * 4
    return head, bufs


def first(place, order, mask, own, toks, share):
    groups, size = own.shape[0] // 2, own.shape[-1]
    rows, keys = groups * share, groups * toks
    head, bufs = scratch(2, groups, toks, share, size)
    shapes = [jax.ShapeDtypeStruct(s, jnp.float32) for s in state_of(2, rows, size)]
    shapes.append(jax.ShapeDtypeStruct((2, size + 16, keys), jnp.bfloat16))
    return pl.pallas_call(
        functools.partial(first_kernel, toks=toks, share=share),
        out_shape=shapes,
        in_specs=[SMEM, SMEM, SMEM, VMEM],
        out_specs=[VMEM] * 4,
        scratch_shapes=head + bufs,
        compiler_params=pltpu.CompilerParams(vmem_limit_bytes=LIMIT),
        cost_estimate=pl.CostEstimate(
            flops=3 * 4 * rows * keys * size,
            bytes_accessed=8 * 2**20,
            transcendentals=3 * rows * keys,
        ),
    )(place, order, mask, own)


def rest(place, order, levels, mask, own, other, gates, state, toks, share):
    groups, size = own.shape[0] // 2, own.shape[-1]
    rows, keys = groups * share, groups * toks
    head, bufs = scratch(4, groups, toks, share, size)
    lists = [
        pltpu.SMEM((17,), jnp.int32),
        pltpu.SMEM((17,), jnp.int32),
        pltpu.SemaphoreType.DMA((6,)),
        pltpu.VMEM((2, groups, share, size), jnp.bfloat16),
        pltpu.VMEM((2, groups, toks, size), jnp.bfloat16),
    ]
    mine = [pltpu.VMEM((4, size + 16, keys), jnp.bfloat16)]
    mine += [pltpu.VMEM(s, jnp.float32) for s in state_of(4, rows, size)]
    return pl.pallas_call(
        functools.partial(rest_kernel, toks=toks, share=share),
        out_shape=jax.ShapeDtypeStruct((4, groups, share, size), jnp.bfloat16),
        in_specs=[SMEM] * 4 + [VMEM, pl.BlockSpec(memory_space=pl.ANY)] + [VMEM] * 5,
        out_specs=VMEM,
        scratch_shapes=lists + head + mine + bufs,
        compiler_params=pltpu.CompilerParams(vmem_limit_bytes=LIMIT),
    )(place, order, levels, mask, own, other, gates, *state)


def shards(queries, keys, values, gate_table, noise_level, stretch_order, block_mask):
    toks, heads, size = queries.shape[1:]
    share = toks // 4
    own = lax.all_to_all(pack(queries[0], keys[0], values[0]), ("xh", "ctx"), 0, 0, tiled=True)
    other = lax.ppermute(own, "core", SWAP)
    place = jnp.stack([lax.axis_index("core"), lax.axis_index("ctx")]).astype(jnp.int32)
    state = first(place, stretch_order, block_mask, own, toks, share)
    part = rest(
        place, stretch_order, noise_level, block_mask, own, other, gate_table, state, toks, share
    )
    back = lax.all_to_all(
        part.reshape(4 * heads, share, size), ("xh", "core", "ctx"), 0, 0, tiled=True
    )
    back = back.reshape(4, heads, share, size)
    return jnp.swapaxes(back, 1, 2).reshape(1, toks, heads, size)


def solution(mesh):
    wide = Mesh(mesh.devices.reshape(2, 2, -1), ("xh", "core", "ctx"))
    tokens = P(("xh", "core"), "ctx", None, None)
    return jax.shard_map(
        shards,
        mesh=wide,
        in_specs=(tokens, tokens, tokens, P(), P(), P(), P()),
        out_specs=tokens,
        check_vma=False,
    )
```

```python
import functools

import jax
import jax.numpy as jnp
from jax import lax
from jax.experimental import pallas as pl
from jax.experimental.pallas import tpu as pltpu
from jax.sharding import Mesh, PartitionSpec as P

LOG2E = 1.4426950408889634
SWAP = [(0, 1), (1, 0)]
BOTH = (((1,), (1,)), ((), ()))
TILE = 512
MIX_TILE = 256
SMEM = pl.BlockSpec(memory_space=pltpu.SMEM)
VMEM = pl.BlockSpec(memory_space=pltpu.VMEM)
LIMIT = 48 * 2**20


def pack_kernel(queries, keys, values, send, q_in, k_in, v_in, wide, q_out, k_out, v_out, ins, outs):
    toks, heads, size = queries.shape
    half = toks // 2
    pitch = wide.shape[1] // toks
    parts = ((keys, k_in, k_out), (values, v_in, v_out), (queries, q_in, q_out))
    loads, stores = [], []
    for i, (src, dst, _) in enumerate(parts):
        for h in range(2):
            at = pl.ds(h * half, half)
            loads.append(pltpu.make_async_copy(src.at[at], dst.at[at], ins.at[2 * i + h]))
            loads[-1].start()
    for i, (_, part, turned) in enumerate(parts):
        for h in range(2):
            loads[2 * i + h].wait()
            for tok in range(h * half, (h + 1) * half):
                wide[i, tok * pitch : tok * pitch + heads, :] = part[tok].astype(jnp.float32)
        for head in range(heads):
            x = wide[i, pl.ds(head, toks, stride=pitch), :].astype(jnp.bfloat16)
            if i < 2:
                turned[head] = x
            else:
                turned[0, head] = x[:half]
                turned[1, head] = x[half:]
        for xh in range(2):
            src = turned if i < 2 else turned.at[xh]
            rows = pl.ds(i * toks, toks if i < 2 else half)
            dst = send.at[pl.ds(xh * heads, heads), rows]
            stores.append(pltpu.make_async_copy(src, dst, outs.at[2 * i + xh]))
            stores[-1].start()
    for copy in stores:
        copy.wait()


def pack(queries, keys, values):
    toks, heads, size = queries.shape
    hbm = pl.BlockSpec(memory_space=pl.ANY)
    block = pltpu.VMEM((toks, heads, size), jnp.bfloat16)
    turned = pltpu.VMEM((heads, toks, size), jnp.bfloat16)
    return pl.pallas_call(
        pack_kernel,
        out_shape=jax.ShapeDtypeStruct((2 * heads, 2 * toks + toks // 2, size), jnp.bfloat16),
        in_specs=[hbm, hbm, hbm],
        out_specs=hbm,
        scratch_shapes=[
            block,
            block,
            block,
            pltpu.VMEM((3, toks * (heads + 1), size), jnp.float32),
            pltpu.VMEM((2, heads, toks // 2, size), jnp.bfloat16),
            turned,
            turned,
            pltpu.SemaphoreType.DMA((6,)),
            pltpu.SemaphoreType.DMA((6,)),
        ],
        compiler_params=pltpu.CompilerParams(vmem_limit_bytes=60 * 2**20),
    )(queries, keys, values)


def stretch_of(slot, core):
    return 2 * (slot % 2) + jnp.where(slot < 2, core, 1 - core)


def load_queries(q, slot, q_all):
    groups, share, size = q.shape
    q_all[slot] = q.reshape(groups * share, size)


def load_own(own, core, toks, share, q_all, k_all):
    groups = own.shape[0] // 2
    start = pl.multiple_of(2 * toks + core * share, 16)
    for slot in range(2):
        at = slice(slot * groups, (slot + 1) * groups)
        load_queries(own[at, pl.ds(start, share), :], slot, q_all)
        k_all[slot] = own[at, 0:toks, :]


def turn(v):
    groups, toks, size = v.shape
    return v.reshape(groups * toks, size).T


def make_step(q_all, k_all, v_all, state, keys):
    run_max, total, mixed = state
    rows, size = q_all.shape[1], k_all.shape[-1]
    toks = k_all.shape[2]
    scale = LOG2E / size**0.5

    def step(fresh, new, used, old):
        best = acc = None
        if used is not None:
            s_old, m_old, f_old = old
            now_q, now_k = used
            m, f = m_old[0:1, :], f_old[0:1, :]
        if fresh is not None:
            s_new, m_new, f_new = new
            next_q, next_k = fresh
            q = q_all[next_q]
        for base in range(0, keys, TILE):
            if fresh is not None:
                k = k_all[next_k, base // toks : (base + TILE) // toks].reshape(TILE, size)
                s = lax.dot_general(k, q, BOTH, preferred_element_type=jnp.float32)
                s_new[base : base + TILE, :] = s
                top = jnp.max(s.reshape(TILE // 8, 8, rows), axis=0)
                best = top if best is None else jnp.maximum(best, top)
            if used is not None:
                for c in range(base, base + TILE, MIX_TILE):
                    p = jnp.exp2(s_old[c : c + MIX_TILE, :] * scale - m)
                    d = jnp.dot(
                        v_all[now_k, :, c : c + MIX_TILE],
                        p.astype(jnp.bfloat16),
                        preferred_element_type=jnp.float32,
                    )
                    acc = d if acc is None else acc + d
        if used is not None:
            total[now_q] = total[now_q] * f + acc[size : size + 8]
            mixed[now_q] = mixed[now_q] * f + acc[:size]
        if fresh is not None:
            before = run_max[next_q]
            after = jnp.maximum(before, jnp.max(best, axis=0, keepdims=True))
            run_max[next_q] = after
            m_new[...] = after * scale
            f_new[...] = jnp.exp2((before - after) * scale)

    return step


def clear(run_max, total, mixed):
    run_max[...] = jnp.full(run_max.shape, -1e30, jnp.float32)
    total[...] = jnp.zeros(total.shape, jnp.float32)
    mixed[...] = jnp.zeros(mixed.shape, jnp.float32)


def first_kernel(
    place, order, mask, own, run_max, total, mixed, v_all, q_all, k_all, *bufs, toks, share
):
    core = place[0]
    groups, size = own.shape[0] // 2, own.shape[-1]
    clear(run_max, total, mixed)
    load_own(own, core, toks, share, q_all, k_all)
    step = make_step(q_all, k_all, v_all, (run_max, total, mixed), groups * toks)
    a, b = bufs[0::2], bufs[1::2]
    v_all[:, size:] = jnp.ones((2, 16, groups * toks), jnp.bfloat16)
    step((0, 0), a, None, None)
    for slot in range(2):
        v_all[slot, :size] = turn(own[slot * groups : (slot + 1) * groups, toks : 2 * toks, :])
    step((1, 1), b, (0, 0), a)
    here, there = order[stretch_of(0, core)], order[stretch_of(1, core)]
    later = jnp.where(here > there, 0, 1)
    cross = (later, 1 - later)
    crossed = mask[jnp.maximum(here, there), jnp.minimum(here, there)] == 1

    @pl.when(crossed)
    def _():
        step(cross, a, (1, 1), b)
        step(None, None, cross, a)

    @pl.when(jnp.logical_not(crossed))
    def _():
        step(None, None, (1, 1), b)


def rest_kernel(
    place, order, levels, mask, own, other, gates, max_in, total_in, mixed_in, v_in, out,
    pair_q, pair_k, sems, q_raw, v_raw, q_all, k_all, v_all, run_max, total, mixed, *bufs, toks, share
):
    core, head = place[0], place[1]
    groups, size = own.shape[0] // 2, own.shape[-1]
    start = pl.multiple_of(2 * toks + core * share, 16)
    copies = []
    for slot in range(2):
        at = pl.ds(slot * groups, groups)
        for rows, dst in (
            (pl.ds(0, toks), k_all.at[2 + slot]),
            (pl.ds(start, share), q_raw.at[slot]),
            (pl.ds(toks, toks), v_raw.at[slot]),
        ):
            copy = pltpu.make_async_copy(other.at[at, rows], dst, sems.at[len(copies)])
            copy.start()
            copies.append(copy)
    clear(run_max.at[2:4], total.at[2:4], mixed.at[2:4])
    run_max[0:2] = max_in[...]
    total[0:2] = total_in[...]
    mixed[0:2] = mixed_in[...]
    v_all[0:2] = v_in[...]
    load_own(own, core, toks, share, q_all, k_all)

    count = jnp.int32(0)
    slots = [(2, 2)] + [(q, k) for k in range(4) for q in range(4) if max(q, k) > 1]
    for i, (query_slot, key_slot) in enumerate(slots):
        pair_q[count] = query_slot
        pair_k[count] = key_slot
        query_pos = order[stretch_of(query_slot, core)]
        key_pos = order[stretch_of(key_slot, core)]
        fits = mask[query_pos, key_pos] == 1
        if i == 0:
            fits = jnp.bool_(True)
        elif (query_slot, key_slot) == (2, 2):
            fits = jnp.bool_(False)
        count = count + fits.astype(jnp.int32)

    step = make_step(q_all, k_all, v_all, (run_max, total, mixed), groups * toks)
    a, b = bufs[0::2], bufs[1::2]

    def pair(n):
        return pair_q[n], pair_k[n]

    for copy in copies[0:2]:
        copy.wait()
    load_queries(q_raw[0], 2, q_all)
    v_all[2:4, size:] = jnp.ones((2, 16, groups * toks), jnp.bfloat16)
    step((2, 2), a, None, None)
    for copy in copies[2:]:
        copy.wait()
    load_queries(q_raw[1], 3, q_all)
    for slot in range(2):
        v_all[2 + slot, :size] = turn(v_raw[slot])

    steps = count - 1

    @pl.loop(0, steps // 2)
    def _(t):
        step(pair(2 * t + 1), b, pair(2 * t), a)
        step(pair(2 * t + 2), a, pair(2 * t + 1), b)

    @pl.when(steps % 2 == 1)
    def _():
        step(pair(steps), b, pair(steps - 1), a)
        step(None, None, pair(steps), b)

    @pl.when(steps % 2 == 0)
    def _():
        step(None, None, pair(steps), a)

    for slot in range(4):
        stretch = stretch_of(slot, core)
        gate = gates[levels[stretch], pl.ds(head, 1), :]
        o = mixed[slot] / total[slot, 0:1, :]
        out[stretch] = (o.T * gate).astype(jnp.bfloat16).reshape(groups, share, size)


def state_of(n, rows, size):
    return [(n, 8, rows), (n, 8, rows), (n, size, rows)]


def scratch(n, groups, toks, share, size):
    f32, bf16 = jnp.float32, jnp.bfloat16
    rows, keys = groups * share, groups * toks
    head = [pltpu.VMEM((n, rows, size), bf16), pltpu.VMEM((n, groups, toks, size), bf16)]
    bufs = [pltpu.VMEM((keys, rows), f32)] * 2 + [pltpu.VMEM((8, rows), f32)] * 4
    return head, bufs


def first(place, order, mask, own, toks, share):
    groups, size = own.shape[0] // 2, own.shape[-1]
    rows, keys = groups * share, groups * toks
    head, bufs = scratch(2, groups, toks, share, size)
    shapes = [jax.ShapeDtypeStruct(s, jnp.float32) for s in state_of(2, rows, size)]
    shapes.append(jax.ShapeDtypeStruct((2, size + 16, keys), jnp.bfloat16))
    return pl.pallas_call(
        functools.partial(first_kernel, toks=toks, share=share),
        out_shape=shapes,
        in_specs=[SMEM, SMEM, SMEM, VMEM],
        out_specs=[VMEM] * 4,
        scratch_shapes=head + bufs,
        compiler_params=pltpu.CompilerParams(vmem_limit_bytes=LIMIT),
        cost_estimate=pl.CostEstimate(
            flops=3 * 4 * rows * keys * size,
            bytes_accessed=8 * 2**20,
            transcendentals=3 * rows * keys,
        ),
    )(place, order, mask, own)


def rest(place, order, levels, mask, own, other, gates, state, toks, share):
    groups, size = own.shape[0] // 2, own.shape[-1]
    rows, keys = groups * share, groups * toks
    head, bufs = scratch(4, groups, toks, share, size)
    lists = [
        pltpu.SMEM((17,), jnp.int32),
        pltpu.SMEM((17,), jnp.int32),
        pltpu.SemaphoreType.DMA((6,)),
        pltpu.VMEM((2, groups, share, size), jnp.bfloat16),
        pltpu.VMEM((2, groups, toks, size), jnp.bfloat16),
    ]
    mine = [pltpu.VMEM((4, size + 16, keys), jnp.bfloat16)]
    mine += [pltpu.VMEM(s, jnp.float32) for s in state_of(4, rows, size)]
    return pl.pallas_call(
        functools.partial(rest_kernel, toks=toks, share=share),
        out_shape=jax.ShapeDtypeStruct((4, groups, share, size), jnp.bfloat16),
        in_specs=[SMEM] * 4 + [VMEM, pl.BlockSpec(memory_space=pl.ANY)] + [VMEM] * 5,
        out_specs=VMEM,
        scratch_shapes=lists + head + mine + bufs,
        compiler_params=pltpu.CompilerParams(vmem_limit_bytes=LIMIT),
    )(place, order, levels, mask, own, other, gates, *state)


def shards(queries, keys, values, gate_table, noise_level, stretch_order, block_mask):
    toks, heads, size = queries.shape[1:]
    share = toks // 4
    own = lax.all_to_all(pack(queries[0], keys[0], values[0]), ("xh", "ctx"), 0, 0, tiled=True)
    other = lax.ppermute(own, "core", SWAP)
    place = jnp.stack([lax.axis_index("core"), lax.axis_index("ctx")]).astype(jnp.int32)
    state = first(place, stretch_order, block_mask, own, toks, share)
    part = rest(
        place, stretch_order, noise_level, block_mask, own, other, gate_table, state, toks, share
    )
    back = lax.all_to_all(
        part.reshape(4 * heads, share, size), ("xh", "core", "ctx"), 0, 0, tiled=True
    )
    back = back.reshape(4, heads, share, size)
    return jnp.swapaxes(back, 1, 2).reshape(1, toks, heads, size)


def solution(mesh):
    wide = Mesh(mesh.devices.reshape(2, 2, -1), ("xh", "core", "ctx"))
    tokens = P(("xh", "core"), "ctx", None, None)
    return jax.shard_map(
        shards,
        mesh=wide,
        in_specs=(tokens, tokens, tokens, P(), P(), P(), P()),
        out_specs=tokens,
        check_vma=False,
    )
```

```python
import functools

import jax
import jax.numpy as jnp
from jax import lax
from jax.experimental import pallas as pl
from jax.experimental.pallas import tpu as pltpu
from jax.sharding import Mesh, PartitionSpec as P

LOG2E = 1.4426950408889634
SWAP = [(0, 1), (1, 0)]
BOTH = (((1,), (1,)), ((), ()))
TILE = 512
MIX_TILE = 256
SMEM = pl.BlockSpec(memory_space=pltpu.SMEM)
VMEM = pl.BlockSpec(memory_space=pltpu.VMEM)
LIMIT = 48 * 2**20


def pack_kernel(queries, keys, values, send, q_in, k_in, v_in, wide, q_out, k_out, v_out, ins, outs):
    toks, heads, size = queries.shape
    half = toks // 2
    pitch = wide.shape[1] // toks
    parts = ((keys, k_in, k_out), (values, v_in, v_out), (queries, q_in, q_out))
    loads, stores = [], []
    for i, (src, dst, _) in enumerate(parts):
        for h in range(2):
            at = pl.ds(h * half, half)
            loads.append(pltpu.make_async_copy(src.at[at], dst.at[at], ins.at[2 * i + h]))
            loads[-1].start()
    for i, (_, part, turned) in enumerate(parts):
        for h in range(2):
            loads[2 * i + h].wait()
            for tok in range(h * half, (h + 1) * half):
                wide[i, tok * pitch : tok * pitch + heads, :] = part[tok].astype(jnp.float32)
        for head in range(heads):
            x = wide[i, pl.ds(head, toks, stride=pitch), :].astype(jnp.bfloat16)
            if i < 2:
                turned[head] = x
            else:
                turned[0, head] = x[:half]
                turned[1, head] = x[half:]
        for xh in range(2):
            src = turned if i < 2 else turned.at[xh]
            rows = pl.ds(i * toks, toks if i < 2 else half)
            dst = send.at[pl.ds(xh * heads, heads), rows]
            stores.append(pltpu.make_async_copy(src, dst, outs.at[2 * i + xh]))
            stores[-1].start()
    for copy in stores:
        copy.wait()


def pack(queries, keys, values):
    toks, heads, size = queries.shape
    hbm = pl.BlockSpec(memory_space=pl.ANY)
    block = pltpu.VMEM((toks, heads, size), jnp.bfloat16)
    turned = pltpu.VMEM((heads, toks, size), jnp.bfloat16)
    return pl.pallas_call(
        pack_kernel,
        out_shape=jax.ShapeDtypeStruct((2 * heads, 2 * toks + toks // 2, size), jnp.bfloat16),
        in_specs=[hbm, hbm, hbm],
        out_specs=hbm,
        scratch_shapes=[
            block,
            block,
            block,
            pltpu.VMEM((3, toks * (heads + 1), size), jnp.float32),
            pltpu.VMEM((2, heads, toks // 2, size), jnp.bfloat16),
            turned,
            turned,
            pltpu.SemaphoreType.DMA((6,)),
            pltpu.SemaphoreType.DMA((6,)),
        ],
        compiler_params=pltpu.CompilerParams(vmem_limit_bytes=60 * 2**20),
    )(queries, keys, values)


def stretch_of(slot, core):
    return 2 * (slot % 2) + jnp.where(slot < 2, core, 1 - core)


def load_queries(q, slot, q_all):
    groups, share, size = q.shape
    q_all[slot] = q.reshape(groups * share, size)


def load_own(own, core, toks, share, q_all, k_all):
    groups = own.shape[0] // 2
    start = pl.multiple_of(2 * toks + core * share, 16)
    for slot in range(2):
        at = slice(slot * groups, (slot + 1) * groups)
        load_queries(own[at, pl.ds(start, share), :], slot, q_all)
        k_all[slot] = own[at, 0:toks, :]


def turn(v):
    groups, toks, size = v.shape
    return v.reshape(groups * toks, size).T


def make_step(q_all, k_all, v_all, state, keys):
    run_max, total, mixed = state
    rows, size = q_all.shape[1], k_all.shape[-1]
    toks = k_all.shape[2]
    scale = LOG2E / size**0.5

    def step(fresh, new, used, old):
        best = acc = None
        if used is not None:
            s_old, m_old, f_old = old
            now_q, now_k = used
            m, f = m_old[0:1, :], f_old[0:1, :]
        if fresh is not None:
            s_new, m_new, f_new = new
            next_q, next_k = fresh
            q = q_all[next_q]
        for base in range(0, keys, TILE):
            if fresh is not None:
                k = k_all[next_k, base // toks : (base + TILE) // toks].reshape(TILE, size)
                s = lax.dot_general(k, q, BOTH, preferred_element_type=jnp.float32)
                s_new[base : base + TILE, :] = s
                top = jnp.max(s.reshape(TILE // 8, 8, rows), axis=0)
                best = top if best is None else jnp.maximum(best, top)
            if used is not None:
                for c in range(base, base + TILE, MIX_TILE):
                    p = jnp.exp2(s_old[c : c + MIX_TILE, :] * scale - m)
                    d = jnp.dot(
                        v_all[now_k, :, c : c + MIX_TILE],
                        p.astype(jnp.bfloat16),
                        preferred_element_type=jnp.float32,
                    )
                    acc = d if acc is None else acc + d
        if used is not None:
            total[now_q] = total[now_q] * f + acc[size : size + 8]
            mixed[now_q] = mixed[now_q] * f + acc[:size]
        if fresh is not None:
            before = run_max[next_q]
            after = jnp.maximum(before, jnp.max(best, axis=0, keepdims=True))
            run_max[next_q] = after
            m_new[...] = after * scale
            f_new[...] = jnp.exp2((before - after) * scale)

    return step


def clear(run_max, total, mixed):
    run_max[...] = jnp.full(run_max.shape, -1e30, jnp.float32)
    total[...] = jnp.zeros(total.shape, jnp.float32)
    mixed[...] = jnp.zeros(mixed.shape, jnp.float32)


def first_kernel(
    place, order, mask, own, run_max, total, mixed, v_all, q_all, k_all, *bufs, toks, share
):
    core = place[0]
    groups, size = own.shape[0] // 2, own.shape[-1]
    clear(run_max, total, mixed)
    load_own(own, core, toks, share, q_all, k_all)
    step = make_step(q_all, k_all, v_all, (run_max, total, mixed), groups * toks)
    a, b = bufs[0::2], bufs[1::2]
    v_all[:, size:] = jnp.ones((2, 16, groups * toks), jnp.bfloat16)
    step((0, 0), a, None, None)
    for slot in range(2):
        v_all[slot, :size] = turn(own[slot * groups : (slot + 1) * groups, toks : 2 * toks, :])
    step((1, 1), b, (0, 0), a)
    here, there = order[stretch_of(0, core)], order[stretch_of(1, core)]
    later = jnp.where(here > there, 0, 1)
    cross = (later, 1 - later)
    crossed = mask[jnp.maximum(here, there), jnp.minimum(here, there)] == 1

    @pl.when(crossed)
    def _():
        step(cross, a, (1, 1), b)
        step(None, None, cross, a)

    @pl.when(jnp.logical_not(crossed))
    def _():
        step(None, None, (1, 1), b)


def rest_kernel(
    place, order, levels, mask, own, other, gates, max_in, total_in, mixed_in, v_in, out,
    pair_q, pair_k, sems, q_raw, v_raw, q_all, k_all, v_all, run_max, total, mixed, *bufs, toks, share
):
    core, head = place[0], place[1]
    groups, size = own.shape[0] // 2, own.shape[-1]
    start = pl.multiple_of(2 * toks + core * share, 16)
    copies = []
    for slot in range(2):
        at = pl.ds(slot * groups, groups)
        for rows, dst in (
            (pl.ds(0, toks), k_all.at[2 + slot]),
            (pl.ds(start, share), q_raw.at[slot]),
            (pl.ds(toks, toks), v_raw.at[slot]),
        ):
            copy = pltpu.make_async_copy(other.at[at, rows], dst, sems.at[len(copies)])
            copy.start()
            copies.append(copy)
    copy = pltpu.make_async_copy(v_in, v_all.at[pl.ds(0, 2)], sems.at[len(copies)])
    copy.start()
    copies.append(copy)
    clear(run_max.at[2:4], total.at[2:4], mixed.at[2:4])
    run_max[0:2] = max_in[...]
    total[0:2] = total_in[...]
    mixed[0:2] = mixed_in[...]
    load_own(own, core, toks, share, q_all, k_all)

    count = jnp.int32(0)
    slots = [(2, 2)] + [(q, k) for k in range(4) for q in range(4) if max(q, k) > 1]
    for i, (query_slot, key_slot) in enumerate(slots):
        pair_q[count] = query_slot
        pair_k[count] = key_slot
        query_pos = order[stretch_of(query_slot, core)]
        key_pos = order[stretch_of(key_slot, core)]
        fits = mask[query_pos, key_pos] == 1
        if i == 0:
            fits = jnp.bool_(True)
        elif (query_slot, key_slot) == (2, 2):
            fits = jnp.bool_(False)
        count = count + fits.astype(jnp.int32)

    step = make_step(q_all, k_all, v_all, (run_max, total, mixed), groups * toks)
    a, b = bufs[0::2], bufs[1::2]

    def pair(n):
        return pair_q[n], pair_k[n]

    for copy in copies[0:2]:
        copy.wait()
    load_queries(q_raw[0], 2, q_all)
    v_all[2:4, size:] = jnp.ones((2, 16, groups * toks), jnp.bfloat16)
    step((2, 2), a, None, None)
    for copy in copies[2:]:
        copy.wait()
    load_queries(q_raw[1], 3, q_all)
    for slot in range(2):
        v_all[2 + slot, :size] = turn(v_raw[slot])

    steps = count - 1

    @pl.loop(0, steps // 2)
    def _(t):
        step(pair(2 * t + 1), b, pair(2 * t), a)
        step(pair(2 * t + 2), a, pair(2 * t + 1), b)

    @pl.when(steps % 2 == 1)
    def _():
        step(pair(steps), b, pair(steps - 1), a)
        step(None, None, pair(steps), b)

    @pl.when(steps % 2 == 0)
    def _():
        step(None, None, pair(steps), a)

    for slot in range(4):
        stretch = stretch_of(slot, core)
        gate = gates[levels[stretch], pl.ds(head, 1), :]
        o = mixed[slot] / total[slot, 0:1, :]
        out[stretch] = (o.T * gate).astype(jnp.bfloat16).reshape(groups, share, size)


def state_of(n, rows, size):
    return [(n, 8, rows), (n, 8, rows), (n, size, rows)]


def scratch(n, groups, toks, share, size):
    f32, bf16 = jnp.float32, jnp.bfloat16
    rows, keys = groups * share, groups * toks
    head = [pltpu.VMEM((n, rows, size), bf16), pltpu.VMEM((n, groups, toks, size), bf16)]
    bufs = [pltpu.VMEM((keys, rows), f32)] * 2 + [pltpu.VMEM((8, rows), f32)] * 4
    return head, bufs


def first(place, order, mask, own, toks, share):
    groups, size = own.shape[0] // 2, own.shape[-1]
    rows, keys = groups * share, groups * toks
    head, bufs = scratch(2, groups, toks, share, size)
    shapes = [jax.ShapeDtypeStruct(s, jnp.float32) for s in state_of(2, rows, size)]
    shapes.append(jax.ShapeDtypeStruct((2, size + 16, keys), jnp.bfloat16))
    return pl.pallas_call(
        functools.partial(first_kernel, toks=toks, share=share),
        out_shape=shapes,
        in_specs=[SMEM, SMEM, SMEM, VMEM],
        out_specs=[VMEM] * 4,
        scratch_shapes=head + bufs,
        compiler_params=pltpu.CompilerParams(vmem_limit_bytes=LIMIT),
        cost_estimate=pl.CostEstimate(
            flops=3 * 4 * rows * keys * size,
            bytes_accessed=8 * 2**20,
            transcendentals=3 * rows * keys,
        ),
    )(place, order, mask, own)


def rest(place, order, levels, mask, own, other, gates, state, toks, share):
    groups, size = own.shape[0] // 2, own.shape[-1]
    rows, keys = groups * share, groups * toks
    head, bufs = scratch(4, groups, toks, share, size)
    lists = [
        pltpu.SMEM((17,), jnp.int32),
        pltpu.SMEM((17,), jnp.int32),
        pltpu.SemaphoreType.DMA((7,)),
        pltpu.VMEM((2, groups, share, size), jnp.bfloat16),
        pltpu.VMEM((2, groups, toks, size), jnp.bfloat16),
    ]
    mine = [pltpu.VMEM((4, size + 16, keys), jnp.bfloat16)]
    mine += [pltpu.VMEM(s, jnp.float32) for s in state_of(4, rows, size)]
    return pl.pallas_call(
        functools.partial(rest_kernel, toks=toks, share=share),
        out_shape=jax.ShapeDtypeStruct((4, groups, share, size), jnp.bfloat16),
        in_specs=[SMEM] * 4 + [VMEM, pl.BlockSpec(memory_space=pl.ANY)] + [VMEM] * 5,
        out_specs=VMEM,
        scratch_shapes=lists + head + mine + bufs,
        compiler_params=pltpu.CompilerParams(vmem_limit_bytes=LIMIT),
    )(place, order, levels, mask, own, other, gates, *state)


def shards(queries, keys, values, gate_table, noise_level, stretch_order, block_mask):
    toks, heads, size = queries.shape[1:]
    share = toks // 4
    own = lax.all_to_all(pack(queries[0], keys[0], values[0]), ("xh", "ctx"), 0, 0, tiled=True)
    other = lax.ppermute(own, "core", SWAP)
    place = jnp.stack([lax.axis_index("core"), lax.axis_index("ctx")]).astype(jnp.int32)
    state = first(place, stretch_order, block_mask, own, toks, share)
    part = rest(
        place, stretch_order, noise_level, block_mask, own, other, gate_table, state, toks, share
    )
    back = lax.all_to_all(
        part.reshape(4 * heads, share, size), ("xh", "core", "ctx"), 0, 0, tiled=True
    )
    back = back.reshape(4, heads, share, size)
    return jnp.swapaxes(back, 1, 2).reshape(1, toks, heads, size)


def solution(mesh):
    wide = Mesh(mesh.devices.reshape(2, 2, -1), ("xh", "core", "ctx"))
    tokens = P(("xh", "core"), "ctx", None, None)
    return jax.shard_map(
        shards,
        mesh=wide,
        in_specs=(tokens, tokens, tokens, P(), P(), P(), P()),
        out_specs=tokens,
        check_vma=False,
    )
```

```python
import functools

import jax
import jax.numpy as jnp
from jax import lax
from jax.experimental import pallas as pl
from jax.experimental.pallas import tpu as pltpu
from jax.sharding import Mesh, PartitionSpec as P

LOG2E = 1.4426950408889634
SWAP = [(0, 1), (1, 0)]
BOTH = (((1,), (1,)), ((), ()))
TILE = 512
MIX_TILE = 256
SMEM = pl.BlockSpec(memory_space=pltpu.SMEM)
VMEM = pl.BlockSpec(memory_space=pltpu.VMEM)
LIMIT = 48 * 2**20


def pack_kernel(queries, keys, values, send, q_in, k_in, v_in, wide, q_out, k_out, v_out, ins, outs):
    toks, heads, size = queries.shape
    half = toks // 2
    pitch = wide.shape[1] // toks
    parts = ((keys, k_in, k_out), (values, v_in, v_out), (queries, q_in, q_out))
    loads, stores = [], []
    for i, (src, dst, _) in enumerate(parts):
        for h in range(2):
            at = pl.ds(h * half, half)
            loads.append(pltpu.make_async_copy(src.at[at], dst.at[at], ins.at[2 * i + h]))
            loads[-1].start()
    for i, (_, part, turned) in enumerate(parts):
        for h in range(2):
            loads[2 * i + h].wait()
            for tok in range(h * half, (h + 1) * half):
                wide[i, tok * pitch : tok * pitch + heads, :] = part[tok].astype(jnp.float32)
        for head in range(heads):
            x = wide[i, pl.ds(head, toks, stride=pitch), :].astype(jnp.bfloat16)
            if i < 2:
                turned[head] = x
            else:
                turned[0, head] = x[:half]
                turned[1, head] = x[half:]
        for xh in range(2):
            src = turned if i < 2 else turned.at[xh]
            rows = pl.ds(i * toks, toks if i < 2 else half)
            dst = send.at[pl.ds(xh * heads, heads), rows]
            stores.append(pltpu.make_async_copy(src, dst, outs.at[2 * i + xh]))
            stores[-1].start()
    for copy in stores:
        copy.wait()


def pack(queries, keys, values):
    toks, heads, size = queries.shape
    hbm = pl.BlockSpec(memory_space=pl.ANY)
    block = pltpu.VMEM((toks, heads, size), jnp.bfloat16)
    turned = pltpu.VMEM((heads, toks, size), jnp.bfloat16)
    return pl.pallas_call(
        pack_kernel,
        out_shape=jax.ShapeDtypeStruct((2 * heads, 2 * toks + toks // 2, size), jnp.bfloat16),
        in_specs=[hbm, hbm, hbm],
        out_specs=hbm,
        scratch_shapes=[
            block,
            block,
            block,
            pltpu.VMEM((3, toks * (heads + 1), size), jnp.float32),
            pltpu.VMEM((2, heads, toks // 2, size), jnp.bfloat16),
            turned,
            turned,
            pltpu.SemaphoreType.DMA((6,)),
            pltpu.SemaphoreType.DMA((6,)),
        ],
        compiler_params=pltpu.CompilerParams(vmem_limit_bytes=60 * 2**20),
    )(queries, keys, values)


def stretch_of(slot, core):
    return 2 * (slot % 2) + jnp.where(slot < 2, core, 1 - core)


def load_queries(q, slot, q_all):
    groups, share, size = q.shape
    q_all[slot] = q.reshape(groups * share, size)


def load_own(own, core, toks, share, q_all, k_all):
    groups = own.shape[0] // 2
    start = pl.multiple_of(2 * toks + core * share, 16)
    for slot in range(2):
        at = slice(slot * groups, (slot + 1) * groups)
        load_queries(own[at, pl.ds(start, share), :], slot, q_all)
        k_all[slot] = own[at, 0:toks, :]


def turn(v):
    groups, toks, size = v.shape
    return v.reshape(groups * toks, size).T


def make_step(q_all, k_all, v_all, state, keys):
    run_max, total, mixed = state
    rows, size = q_all.shape[1], k_all.shape[-1]
    toks = k_all.shape[2]
    scale = LOG2E / size**0.5

    def step(fresh, new, used, old):
        best = acc = None
        if used is not None:
            s_old, m_old, f_old = old
            now_q, now_k = used
            m, f = m_old[0:1, :], f_old[0:1, :]
        if fresh is not None:
            s_new, m_new, f_new = new
            next_q, next_k = fresh
            q = q_all[next_q]
        for base in range(0, keys, TILE):
            if fresh is not None:
                k = k_all[next_k, base // toks : (base + TILE) // toks].reshape(TILE, size)
                s = lax.dot_general(k, q, BOTH, preferred_element_type=jnp.float32)
                s_new[base : base + TILE, :] = s
                top = jnp.max(s.reshape(TILE // 8, 8, rows), axis=0)
                best = top if best is None else jnp.maximum(best, top)
            if used is not None:
                for c in range(base, base + TILE, MIX_TILE):
                    p = jnp.exp2(s_old[c : c + MIX_TILE, :] * scale - m)
                    d = jnp.dot(
                        v_all[now_k, :, c : c + MIX_TILE],
                        p.astype(jnp.bfloat16),
                        preferred_element_type=jnp.float32,
                    )
                    acc = d if acc is None else acc + d
        if used is not None:
            total[now_q] = total[now_q] * f + acc[size : size + 8]
            mixed[now_q] = mixed[now_q] * f + acc[:size]
        if fresh is not None:
            before = run_max[next_q]
            after = jnp.maximum(before, jnp.max(best, axis=0, keepdims=True))
            run_max[next_q] = after
            m_new[...] = after * scale
            f_new[...] = jnp.exp2((before - after) * scale)

    return step


def clear(run_max, total, mixed):
    run_max[...] = jnp.full(run_max.shape, -1e30, jnp.float32)
    total[...] = jnp.zeros(total.shape, jnp.float32)
    mixed[...] = jnp.zeros(mixed.shape, jnp.float32)


def first_kernel(
    place, order, mask, own, run_max, total, mixed, v_all, q_all, k_all, *bufs, toks, share
):
    core = place[0]
    groups, size = own.shape[0] // 2, own.shape[-1]
    clear(run_max, total, mixed)
    load_own(own, core, toks, share, q_all, k_all)
    step = make_step(q_all, k_all, v_all, (run_max, total, mixed), groups * toks)
    a, b = bufs[0::2], bufs[1::2]
    v_all[:, size:] = jnp.ones((2, 16, groups * toks), jnp.bfloat16)
    step((0, 0), a, None, None)
    for slot in range(2):
        v_all[slot, :size] = turn(own[slot * groups : (slot + 1) * groups, toks : 2 * toks, :])
    step((1, 1), b, (0, 0), a)
    here, there = order[stretch_of(0, core)], order[stretch_of(1, core)]
    later = jnp.where(here > there, 0, 1)
    cross = (later, 1 - later)
    crossed = mask[jnp.maximum(here, there), jnp.minimum(here, there)] == 1

    @pl.when(crossed)
    def _():
        step(cross, a, (1, 1), b)
        step(None, None, cross, a)

    @pl.when(jnp.logical_not(crossed))
    def _():
        step(None, None, (1, 1), b)


def rest_kernel(
    place, order, levels, mask, own, other, gates, max_in, total_in, mixed_in, v_in, out,
    pair_q, pair_k, sems, q_raw, v_raw, q_all, k_all, v_all, run_max, total, mixed, *bufs, toks, share
):
    core, head = place[0], place[1]
    groups, size = own.shape[0] // 2, own.shape[-1]
    start = pl.multiple_of(2 * toks + core * share, 16)
    copies = []
    for slot in range(2):
        at = pl.ds(slot * groups, groups)
        for rows, dst in (
            (pl.ds(0, toks), k_all.at[2 + slot]),
            (pl.ds(start, share), q_raw.at[slot]),
            (pl.ds(toks, toks), v_raw.at[slot]),
        ):
            copy = pltpu.make_async_copy(other.at[at, rows], dst, sems.at[len(copies)])
            copy.start()
            copies.append(copy)
    for src, dst in ((v_in, v_all), (mixed_in, mixed)):
        copy = pltpu.make_async_copy(src, dst.at[pl.ds(0, 2)], sems.at[len(copies)])
        copy.start()
        copies.append(copy)
    clear(run_max.at[2:4], total.at[2:4], mixed.at[2:4])
    run_max[0:2] = max_in[...]
    total[0:2] = total_in[...]
    load_own(own, core, toks, share, q_all, k_all)

    count = jnp.int32(0)
    slots = [(2, 2)] + [(q, k) for k in range(4) for q in range(4) if max(q, k) > 1]
    for i, (query_slot, key_slot) in enumerate(slots):
        pair_q[count] = query_slot
        pair_k[count] = key_slot
        query_pos = order[stretch_of(query_slot, core)]
        key_pos = order[stretch_of(key_slot, core)]
        fits = mask[query_pos, key_pos] == 1
        if i == 0:
            fits = jnp.bool_(True)
        elif (query_slot, key_slot) == (2, 2):
            fits = jnp.bool_(False)
        count = count + fits.astype(jnp.int32)

    step = make_step(q_all, k_all, v_all, (run_max, total, mixed), groups * toks)
    a, b = bufs[0::2], bufs[1::2]

    def pair(n):
        return pair_q[n], pair_k[n]

    for copy in copies[0:2]:
        copy.wait()
    load_queries(q_raw[0], 2, q_all)
    v_all[2:4, size:] = jnp.ones((2, 16, groups * toks), jnp.bfloat16)
    step((2, 2), a, None, None)
    for copy in copies[2:]:
        copy.wait()
    load_queries(q_raw[1], 3, q_all)
    for slot in range(2):
        v_all[2 + slot, :size] = turn(v_raw[slot])

    steps = count - 1

    @pl.loop(0, steps // 2)
    def _(t):
        step(pair(2 * t + 1), b, pair(2 * t), a)
        step(pair(2 * t + 2), a, pair(2 * t + 1), b)

    @pl.when(steps % 2 == 1)
    def _():
        step(pair(steps), b, pair(steps - 1), a)
        step(None, None, pair(steps), b)

    @pl.when(steps % 2 == 0)
    def _():
        step(None, None, pair(steps), a)

    for slot in range(4):
        stretch = stretch_of(slot, core)
        gate = gates[levels[stretch], pl.ds(head, 1), :]
        o = mixed[slot] / total[slot, 0:1, :]
        out[stretch] = (o.T * gate).astype(jnp.bfloat16).reshape(groups, share, size)


def state_of(n, rows, size):
    return [(n, 8, rows), (n, 8, rows), (n, size, rows)]


def scratch(n, groups, toks, share, size):
    f32, bf16 = jnp.float32, jnp.bfloat16
    rows, keys = groups * share, groups * toks
    head = [pltpu.VMEM((n, rows, size), bf16), pltpu.VMEM((n, groups, toks, size), bf16)]
    bufs = [pltpu.VMEM((keys, rows), f32)] * 2 + [pltpu.VMEM((8, rows), f32)] * 4
    return head, bufs


def first(place, order, mask, own, toks, share):
    groups, size = own.shape[0] // 2, own.shape[-1]
    rows, keys = groups * share, groups * toks
    head, bufs = scratch(2, groups, toks, share, size)
    shapes = [jax.ShapeDtypeStruct(s, jnp.float32) for s in state_of(2, rows, size)]
    shapes.append(jax.ShapeDtypeStruct((2, size + 16, keys), jnp.bfloat16))
    return pl.pallas_call(
        functools.partial(first_kernel, toks=toks, share=share),
        out_shape=shapes,
        in_specs=[SMEM, SMEM, SMEM, VMEM],
        out_specs=[VMEM] * 4,
        scratch_shapes=head + bufs,
        compiler_params=pltpu.CompilerParams(vmem_limit_bytes=LIMIT),
        cost_estimate=pl.CostEstimate(
            flops=3 * 4 * rows * keys * size,
            bytes_accessed=8 * 2**20,
            transcendentals=3 * rows * keys,
        ),
    )(place, order, mask, own)


def rest(place, order, levels, mask, own, other, gates, state, toks, share):
    groups, size = own.shape[0] // 2, own.shape[-1]
    rows, keys = groups * share, groups * toks
    head, bufs = scratch(4, groups, toks, share, size)
    lists = [
        pltpu.SMEM((17,), jnp.int32),
        pltpu.SMEM((17,), jnp.int32),
        pltpu.SemaphoreType.DMA((8,)),
        pltpu.VMEM((2, groups, share, size), jnp.bfloat16),
        pltpu.VMEM((2, groups, toks, size), jnp.bfloat16),
    ]
    mine = [pltpu.VMEM((4, size + 16, keys), jnp.bfloat16)]
    mine += [pltpu.VMEM(s, jnp.float32) for s in state_of(4, rows, size)]
    return pl.pallas_call(
        functools.partial(rest_kernel, toks=toks, share=share),
        out_shape=jax.ShapeDtypeStruct((4, groups, share, size), jnp.bfloat16),
        in_specs=[SMEM] * 4 + [VMEM, pl.BlockSpec(memory_space=pl.ANY)] + [VMEM] * 5,
        out_specs=VMEM,
        scratch_shapes=lists + head + mine + bufs,
        compiler_params=pltpu.CompilerParams(vmem_limit_bytes=LIMIT),
    )(place, order, levels, mask, own, other, gates, *state)


def shards(queries, keys, values, gate_table, noise_level, stretch_order, block_mask):
    toks, heads, size = queries.shape[1:]
    share = toks // 4
    own = lax.all_to_all(pack(queries[0], keys[0], values[0]), ("xh", "ctx"), 0, 0, tiled=True)
    other = lax.ppermute(own, "core", SWAP)
    place = jnp.stack([lax.axis_index("core"), lax.axis_index("ctx")]).astype(jnp.int32)
    state = first(place, stretch_order, block_mask, own, toks, share)
    part = rest(
        place, stretch_order, noise_level, block_mask, own, other, gate_table, state, toks, share
    )
    back = lax.all_to_all(
        part.reshape(4 * heads, share, size), ("xh", "core", "ctx"), 0, 0, tiled=True
    )
    back = back.reshape(4, heads, share, size)
    return jnp.swapaxes(back, 1, 2).reshape(1, toks, heads, size)


def solution(mesh):
    wide = Mesh(mesh.devices.reshape(2, 2, -1), ("xh", "core", "ctx"))
    tokens = P(("xh", "core"), "ctx", None, None)
    return jax.shard_map(
        shards,
        mesh=wide,
        in_specs=(tokens, tokens, tokens, P(), P(), P(), P()),
        out_specs=tokens,
        check_vma=False,
    )
```
